32 devices in a mesh: span: 4 (over y, x), ty: 2 (over core), tx: 4 (over z).
Axes of the slice: x: 2, y: 2, z: 4, core: 2. Of those that a mesh axis runs over, the one named last changes fastest.
Arguments:
- queries: bfloat16 [4, 2, 4, 128, 1536], P('span', 'ty', 'tx'), may hold values from -125 to 125
- key_value: bfloat16 [4, 2, 4, 128, 1024], P('span', 'ty', 'tx'), may hold values from -5 to 5
- pattern: int32 [4, 2, 4, 5], P('span', 'ty', 'tx'), may hold values from 0 to 1
- counts: int32 [4, 2, 4], replicated, may hold values from 64 to 128, as said below
- span_mask: int32 [4, 4], replicated, may hold values from 0 to 1, as said below
Outputs:
- attended: bfloat16 [4, 2, 4, 128, 1536], P('span', 'ty', 'tx')
The draws below stay inside these ranges and needn't reach their ends.
Inputs may be any that keep to these rules, and one draw needn't show every extreme that they name: `counts`: in every span some tile has all 128 slots valid. span_mask[c, c] is 1 and span_mask[c, c'] is 0 for c' > c.
All inputs are finite; a program needn't handle non-finite values.
Results may differ from the reference program's by a relative error of at most 0.006.
Values may be sent and summed in bfloat16 or wider, within the bound.
No kernel may reach another device: no remote copies, remote signals or barrier semaphores. Data moves between devices by JAX's collectives and lax.ppermute only.
A program may use at most 64 MiB of HBM per device.

```python
import math
import jax
import jax.numpy as jnp
from jax import lax

HEAD_SIZE = 128
KEY_VALUE_HEADS = 4
QUERY_PER_KV = 3
NEIGH = 5
TOKEN_SLOTS = 128
SPAN_COUNT = 4
TILE_ROWS = 2
TILE_COLUMNS = 4


def base_keys(key):
    key_sampler = jax.random.normal(jax.random.fold_in(key, 101), (SPAN_COUNT, TILE_ROWS, TILE_COLUMNS, TOKEN_SLOTS, KEY_VALUE_HEADS, HEAD_SIZE), jnp.float32)
    return jnp.clip(key_sampler, -5.0, 5.0)


def draw_key_value(key, part):
    key_sampler = base_keys(key)
    complete_shape = (SPAN_COUNT, TILE_ROWS, TILE_COLUMNS, TOKEN_SLOTS, KEY_VALUE_HEADS, HEAD_SIZE)
    value_matrix = jnp.clip(jax.random.normal(jax.random.fold_in(key, 102), complete_shape, jnp.float32), -5.0, 5.0)
    packed_rows = jnp.concatenate([key_sampler.reshape(SPAN_COUNT, TILE_ROWS, TILE_COLUMNS, TOKEN_SLOTS, KEY_VALUE_HEADS * HEAD_SIZE), value_matrix.reshape(SPAN_COUNT, TILE_ROWS, TILE_COLUMNS, TOKEN_SLOTS, KEY_VALUE_HEADS * HEAD_SIZE)], axis=-1)
    return packed_rows.astype(jnp.bfloat16)


def draw_queries(key, part):
    complete_shape = (SPAN_COUNT, TILE_ROWS, TILE_COLUMNS, TOKEN_SLOTS, KEY_VALUE_HEADS, QUERY_PER_KV, HEAD_SIZE)
    sampled_blocks = jnp.clip(jax.random.normal(jax.random.fold_in(key, 103), complete_shape, jnp.float32), -5.0, 5.0)
    return sampled_blocks.reshape(SPAN_COUNT, TILE_ROWS, TILE_COLUMNS, TOKEN_SLOTS, KEY_VALUE_HEADS * QUERY_PER_KV * HEAD_SIZE).astype(jnp.bfloat16)


def draw_pattern(key, part):
    opened = (jax.random.randint(jax.random.fold_in(key, 104), (SPAN_COUNT, TILE_ROWS, TILE_COLUMNS, NEIGH), 0, 4) > 0).astype(jnp.int32)
    return opened.at[..., 0].set(1)


def draw_counts(key, part):
    filled = jax.random.randint(jax.random.fold_in(key, 105), (SPAN_COUNT, TILE_ROWS * TILE_COLUMNS), TOKEN_SLOTS // 2, TOKEN_SLOTS + 1)
    fullest = jax.random.randint(jax.random.fold_in(key, 106), (SPAN_COUNT,), 0, TILE_ROWS * TILE_COLUMNS)
    filled = filled.at[jnp.arange(SPAN_COUNT), fullest].set(TOKEN_SLOTS)
    return filled.reshape(SPAN_COUNT, TILE_ROWS, TILE_COLUMNS).astype(jnp.int32)


def draw_span_mask(key, part):
    bits_drawn = (jax.random.randint(jax.random.fold_in(key, 107), (SPAN_COUNT, SPAN_COUNT), 0, 4) > 0).astype(jnp.int32)
    row_ids = jnp.arange(SPAN_COUNT)[:, None]
    col_ids = jnp.arange(SPAN_COUNT)[None, :]
    return jnp.where(row_ids > col_ids, bits_drawn, jnp.where(row_ids == col_ids, 1, 0)).astype(jnp.int32)


def setup_inputs(seed: int = 0) -> dict:
    keys = jax.random.split(jax.random.key(seed), 6)
    return {
        "queries": draw_queries(jax.random.fold_in(keys[5], 71), 0),
        "key_value": draw_key_value(jax.random.fold_in(keys[5], 71), 0),
        "pattern": draw_pattern(jax.random.fold_in(keys[5], 71), 0),
        "counts": draw_counts(jax.random.fold_in(keys[5], 71), 0),
        "span_mask": draw_span_mask(jax.random.fold_in(keys[5], 71), 0),
    }


OFFSETS = ((0, 0), (-1, 0), (1, 0), (0, -1), (0, 1))

def as_index(value):
    return jnp.asarray(value).astype(jnp.int32)

def reference(queries, key_value, pattern, counts, span_mask):
    window_radius = KEY_VALUE_HEADS * HEAD_SIZE
    scale = 1.0 / math.sqrt(HEAD_SIZE)
    ext_kv = jnp.pad(key_value, ((0, 0), (1, 1), (1, 1), (0, 0), (0, 0)))
    ext_counts = jnp.pad(counts, ((0, 0), (1, 1), (1, 1)))
    flat_query = queries.reshape(SPAN_COUNT * TILE_ROWS * TILE_COLUMNS, TOKEN_SLOTS, KEY_VALUE_HEADS, QUERY_PER_KV, HEAD_SIZE)
    flat_pattern = pattern.reshape(SPAN_COUNT * TILE_ROWS * TILE_COLUMNS, NEIGH)
    row_ids = jnp.arange(TOKEN_SLOTS, dtype=jnp.int32)
    zero_index = as_index(0)

    def one_tile(tile_index):
        span_id = as_index(tile_index // (TILE_ROWS * TILE_COLUMNS))
        tile_y = as_index(tile_index // TILE_COLUMNS % TILE_ROWS)
        tile_x = as_index(tile_index % TILE_COLUMNS)
        kv_pieces = []
        alive_list = []
        for shift_y, shift_x in OFFSETS:
            start_y = as_index(tile_y + (1 + shift_y))
            start_x = as_index(tile_x + (1 + shift_x))
            piece_kv = lax.dynamic_slice(ext_kv, (zero_index, start_y, start_x, zero_index, zero_index), (SPAN_COUNT, 1, 1, TOKEN_SLOTS, 2 * window_radius))
            kv_pieces.append(piece_kv.reshape(SPAN_COUNT, TOKEN_SLOTS, 2 * window_radius))
            piece_count = lax.dynamic_slice(ext_counts, (zero_index, start_y, start_x), (SPAN_COUNT, 1, 1)).reshape(SPAN_COUNT)
            alive_list.append(row_ids[None, :] < piece_count[:, None])
        key_value_block = jnp.stack(kv_pieces, axis=1)
        alive_keys = jnp.stack(alive_list, axis=1)
        opened = lax.dynamic_index_in_dim(flat_pattern, tile_index, 0, keepdims=False) > 0
        causal = lax.dynamic_index_in_dim(span_mask, span_id, 0, keepdims=False) > 0
        alive_keys = (alive_keys & opened[None, :, None] & causal[:, None, None]).reshape(-1)
        key_matrix = key_value_block[..., :window_radius].reshape(-1, KEY_VALUE_HEADS, HEAD_SIZE).astype(jnp.float32)
        value_matrix = key_value_block[..., window_radius:].reshape(-1, KEY_VALUE_HEADS, HEAD_SIZE).astype(jnp.float32)
        query_rows = lax.dynamic_index_in_dim(flat_query, tile_index, 0, keepdims=False).astype(jnp.float32)
        scores = jnp.einsum('tkgd,lkd->tkgl', query_rows, key_matrix) * scale
        scores = jnp.where(alive_keys, scores, -1e+30)
        row_max = lax.optimization_barrier(jnp.max(scores, axis=-1, keepdims=True))
        weights = jnp.where(alive_keys, jnp.exp(scores - row_max), 0.0)
        denom_sum = lax.optimization_barrier(jnp.sum(weights, axis=-1))
        rounded = lax.optimization_barrier(weights.astype(jnp.bfloat16)).astype(jnp.float32)
        attended = jnp.einsum('tkgl,lkd->tkgd', rounded, value_matrix) / denom_sum[..., None]
        own_count = ext_counts[span_id, tile_y + 1, tile_x + 1]
        attended = jnp.where(row_ids[:, None, None, None] < own_count, attended, 0.0)
        return attended.reshape(TOKEN_SLOTS, KEY_VALUE_HEADS * QUERY_PER_KV * HEAD_SIZE).astype(jnp.bfloat16)
    final_output = lax.map(one_tile, jnp.arange(SPAN_COUNT * TILE_ROWS * TILE_COLUMNS, dtype=jnp.int32))
    return final_output.reshape(SPAN_COUNT, TILE_ROWS, TILE_COLUMNS, TOKEN_SLOTS, KEY_VALUE_HEADS * QUERY_PER_KV * HEAD_SIZE)
```

```python
import functools

import jax
import jax.numpy as jnp
from jax import lax
from jax.experimental import pallas as pl
from jax.experimental.pallas import tpu as pltpu
from jax.sharding import PartitionSpec as P

HEAD_SIZE = 128
NEIGH = 5
EXTRA = 16
DEAD = -1e30
VMEM_LIMIT = 40 * 1024 * 1024


def vmem():
    return pl.BlockSpec(memory_space=pltpu.VMEM)


def smem():
    return pl.BlockSpec(memory_space=pltpu.SMEM)


def pairings(count):
    found = []
    for first in (0, 1):
        pairs = [(i, i + 1) for i in range(first, count - 1, 2)]
        if pairs:
            found.append(pairs)
    return found


def swap(block, axis, pairs):
    return lax.ppermute(block, axis, pairs + [(b, a) for a, b in pairs])


def partner(place, count, first):
    low = lax.rem(place + first, 2) == 0
    step = jnp.where(low, 1, -1)
    other = place + step
    return jnp.where((other >= 0) & (other < count), step, 0)


def split_kv(spans, kv_ref, *piece_refs):
    me = lax.axis_index("span")
    kv_width = kv_ref.shape[1] // 2
    for k in range(spans):
        head = me ^ k
        for part in range(2):
            start = pl.multiple_of(part * kv_width + head * HEAD_SIZE, HEAD_SIZE)
            piece_refs[k][part] = kv_ref[:, pl.ds(start, HEAD_SIZE)]


def split_q(spans, pattern_ref, q_ref, *piece_refs):
    me = lax.axis_index("span")
    rows = q_ref.shape[0]
    width = q_ref.shape[1] // spans
    row_ids = lax.broadcasted_iota(jnp.int32, (EXTRA, width), 0)
    extra = jnp.zeros((EXTRA, width), jnp.float32)
    for o in range(NEIGH):
        value = pattern_ref[o].astype(jnp.float32)
        extra = jnp.where(row_ids == o, value, extra)
    extra = extra.astype(jnp.bfloat16)
    for k in range(spans):
        start = pl.multiple_of((me ^ k) * width, HEAD_SIZE)
        piece_refs[k][:rows] = q_ref[:, pl.ds(start, width)]
        piece_refs[k][rows:] = extra


def attend(spans, ty_count, tx_count, ways, *refs):
    counts_ref, mask_ref = refs[:2]
    q_refs = refs[2 : 2 + spans]
    tile_refs = refs[2 + spans : 3 + spans + len(ways)]
    out_refs = refs[3 + spans + len(ways) : 3 + 2 * spans + len(ways)]
    score_ref, top_ref, sum_ref, acc_ref = refs[3 + 2 * spans + len(ways) :]
    me, row, col = (lax.axis_index(a) for a in ("span", "ty", "tx"))
    tok_rows = out_refs[0].shape[0]
    groups = out_refs[0].shape[1] // HEAD_SIZE
    scale = HEAD_SIZE ** (-0.5)
    slots = tile_refs[0].shape[2]
    lanes = lax.broadcasted_iota(jnp.int32, (1, slots), 1)

    steps = []
    for axis, first in ways:
        place, count = (row, ty_count) if axis == "ty" else (col, tx_count)
        steps.append(partner(place, count, first))

    def tile_count(span, step_row, step_col):
        index = (span * ty_count + row + step_row) * tx_count + col + step_col
        return counts_ref[index]

    def bias_of(k, other):
        span = me ^ other
        extra = q_refs[k][tok_rows:, :HEAD_SIZE].astype(jnp.float32)
        parts = [jnp.where((lanes < tile_count(span, 0, 0)) & (extra[0:1] > 0), 0.0, DEAD)]
        for (axis, _), step in zip(ways, steps, strict=True):
            base = 1 if axis == "ty" else 3
            chosen = jnp.where(step > 0, extra[base + 1 : base + 2], extra[base : base + 1])
            near = tile_count(span, *((step, 0) if axis == "ty" else (0, step)))
            near = jnp.where(step == 0, 0, near)
            parts.append(jnp.where((lanes < near) & (chosen > 0), 0.0, DEAD))
        return jnp.concatenate(parts, axis=1)

    tiles = 1 + len(ways)
    for k in range(spans):
        span = me ^ k
        query = jnp.concatenate(
            [q_refs[k][:tok_rows, g * HEAD_SIZE : (g + 1) * HEAD_SIZE] for g in range(groups)], axis=0
        )
        top_ref[...] = jnp.full(top_ref.shape, DEAD, jnp.float32)
        sum_ref[...] = jnp.zeros(sum_ref.shape, jnp.float32)
        acc_ref[...] = jnp.zeros(acc_ref.shape, jnp.float32)
        for other in range(spans):

            @pl.when(mask_ref[span * spans + (me ^ other)] > 0)
            def _(other=other):
                keys = jnp.concatenate([t[other, 0] for t in tile_refs], axis=0)
                scores = lax.dot_general(
                    query, keys, (((1,), (1,)), ((), ())), preferred_element_type=jnp.float32
                )
                scores = scores * scale + bias_of(k, other)
                score_ref[other] = scores
                top = top_ref[...]
                for t in range(tiles):
                    top = jnp.maximum(top, scores[:, t * slots : (t + 1) * slots])
                top_ref[...] = top

        top = jnp.max(top_ref[...], axis=1, keepdims=True)
        for other in range(spans):

            @pl.when(mask_ref[span * spans + (me ^ other)] > 0)
            def _(other=other):
                values = jnp.concatenate([t[other, 1] for t in tile_refs], axis=0)
                weights = jnp.exp(score_ref[other] - top)
                total = sum_ref[...]
                for t in range(tiles):
                    total = total + weights[:, t * slots : (t + 1) * slots]
                sum_ref[...] = total
                acc_ref[...] += jnp.dot(
                    weights.astype(jnp.bfloat16), values, preferred_element_type=jnp.float32
                )

        total = jnp.sum(sum_ref[...], axis=1, keepdims=True)
        result = acc_ref[...] / jnp.where(top > 0.5 * DEAD, total, jnp.nan)
        valid = lax.broadcasted_iota(jnp.int32, (tok_rows, HEAD_SIZE), 0) < tile_count(span, 0, 0)
        for g in range(groups):
            part = jnp.where(valid, result[g * tok_rows : (g + 1) * tok_rows], 0.0)
            out_refs[k][:, g * HEAD_SIZE : (g + 1) * HEAD_SIZE] = part.astype(jnp.bfloat16)


def join(spans, *refs):
    me = lax.axis_index("span")
    out_ref = refs[spans]
    width = refs[0].shape[1]
    for k in range(spans):
        start = pl.multiple_of((me ^ k) * width, HEAD_SIZE)
        out_ref[:, pl.ds(start, width)] = refs[k][...]


def shards(queries, key_value, pattern, counts, span_mask):
    spans, ty_count, tx_count = (lax.axis_size(a) for a in ("span", "ty", "tx"))
    tok_rows = queries.shape[3]
    kv_heads = key_value.shape[4] // (2 * HEAD_SIZE)
    assert kv_heads == spans and spans & (spans - 1) == 0
    width = queries.shape[4] // spans
    groups = width // HEAD_SIZE
    bf16 = jnp.bfloat16
    params = pltpu.CompilerParams(vmem_limit_bytes=VMEM_LIMIT)

    def exchange(block, k):
        return lax.ppermute(block, "span", [(i, i ^ k) for i in range(spans)])

    order = sorted(range(1, spans), key=lambda k: -bin(k).count("1"))

    kv_pieces = pl.pallas_call(
        functools.partial(split_kv, spans),
        out_shape=[jax.ShapeDtypeStruct((2, tok_rows, HEAD_SIZE), bf16)] * spans,
        in_specs=[vmem()],
        out_specs=[vmem()] * spans,
        compiler_params=params,
        name="split_kv",
    )(key_value.reshape(tok_rows, -1))
    q_pieces = pl.pallas_call(
        functools.partial(split_q, spans),
        out_shape=[jax.ShapeDtypeStruct((tok_rows + EXTRA, width), bf16)] * spans,
        in_specs=[smem(), vmem()],
        out_specs=[vmem()] * spans,
        compiler_params=params,
        name="split_q",
    )(pattern.reshape(NEIGH), queries.reshape(tok_rows, -1))

    column = [kv_pieces[0]] + [None] * (spans - 1)
    for k in order:
        column[k] = exchange(kv_pieces[k], k)
    own = jnp.stack(column)
    q_here = [q_pieces[0]] + [None] * (spans - 1)
    for k in order:
        q_here[k] = exchange(q_pieces[k], k)

    ways, tiles = [], [own]
    for axis, count in (("tx", tx_count), ("ty", ty_count)):
        for first, pairs in enumerate(pairings(count)):
            ways.append((axis, first))
            tiles.append(swap(own, axis, pairs))

    keys = len(tiles) * tok_rows
    outs = pl.pallas_call(
        functools.partial(attend, spans, ty_count, tx_count, tuple(ways)),
        out_shape=[jax.ShapeDtypeStruct((tok_rows, width), bf16)] * spans,
        in_specs=[smem(), smem()] + [vmem()] * (spans + len(tiles)),
        out_specs=[vmem()] * spans,
        scratch_shapes=[
            pltpu.VMEM((spans, groups * tok_rows, keys), jnp.float32),
            pltpu.VMEM((groups * tok_rows, tok_rows), jnp.float32),
            pltpu.VMEM((groups * tok_rows, tok_rows), jnp.float32),
            pltpu.VMEM((groups * tok_rows, HEAD_SIZE), jnp.float32),
        ],
        compiler_params=params,
        name="attend",
    )(counts.reshape(-1), span_mask.reshape(-1), *q_here, *tiles)

    home = [outs[0]] + [None] * (spans - 1)
    for k in order:
        home[k] = exchange(outs[k], k)
    attended = pl.pallas_call(
        functools.partial(join, spans),
        out_shape=jax.ShapeDtypeStruct((tok_rows, spans * width), bf16),
        in_specs=[vmem()] * spans,
        out_specs=vmem(),
        compiler_params=params,
        name="join",
    )(*home)
    return attended.reshape(1, 1, 1, tok_rows, -1)


def solution(mesh):
    return jax.shard_map(
        shards,
        mesh=mesh,
        in_specs=(
            P("span", "ty", "tx", None, None),
            P("span", "ty", "tx", None, None),
            P("span", "ty", "tx", None),
            P(),
            P(),
        ),
        out_specs=P("span", "ty", "tx", None, None),
        check_vma=False,
    )
```

```python
import functools
import math

import jax
import jax.numpy as jnp
from jax import lax
from jax.experimental import pallas as pl
from jax.experimental.pallas import tpu as pltpu
from jax.sharding import PartitionSpec as P

HEAD_SIZE = 128
NEIGH = 5
EXTRA = 16
CHUNK = 64
NEAR_FLOPS = 1_000_000_000
DEAD = -1e30
VMEM_LIMIT = 40 * 1024 * 1024


def vmem():
    return pl.BlockSpec(memory_space=pltpu.VMEM)


def smem():
    return pl.BlockSpec(memory_space=pltpu.SMEM)


def pairings(count):
    found = []
    for first in (0, 1):
        pairs = [(i, i + 1) for i in range(first, count - 1, 2)]
        if pairs:
            found.append(pairs)
    return found


def swap(block, axis, pairs):
    return lax.ppermute(block, axis, pairs + [(b, a) for a, b in pairs])


def partner(place, count, first):
    low = lax.rem(place + first, 2) == 0
    step = jnp.where(low, 1, -1)
    other = place + step
    return jnp.where((other >= 0) & (other < count), step, 0)


def split(spans, pattern_hbm, kv_hbm, q_hbm, *refs):
    kv_refs, q_refs = refs[:spans], refs[spans : 2 * spans]
    pattern_ref, kv_sem, q_sem, pattern_sem = refs[2 * spans :]
    me = lax.axis_index("span")
    kv_width = kv_hbm.shape[1] // 2
    rows = q_hbm.shape[0]
    width = q_hbm.shape[1] // spans
    copies = [pltpu.make_async_copy(pattern_hbm, pattern_ref, pattern_sem)]
    for k in range(spans):
        head = me ^ k
        for part in range(2):
            start = pl.multiple_of(part * kv_width + head * HEAD_SIZE, HEAD_SIZE)
            copies.append(
                pltpu.make_async_copy(
                    kv_hbm.at[:, pl.ds(start, HEAD_SIZE)], kv_refs[k].at[part], kv_sem.at[k, part]
                )
            )
    for k in range(spans):
        start = pl.multiple_of((me ^ k) * width, HEAD_SIZE)
        copies.append(
            pltpu.make_async_copy(
                q_hbm.at[:, pl.ds(start, width)], q_refs[k].at[pl.ds(0, rows)], q_sem.at[k]
            )
        )
    for copy in copies:
        copy.start()
    copies[0].wait()
    row_ids = lax.broadcasted_iota(jnp.int32, (EXTRA, width), 0)
    extra = jnp.zeros((EXTRA, width), jnp.float32)
    for o in range(NEIGH):
        extra = jnp.where(row_ids == o, pattern_ref[o].astype(jnp.float32), extra)
    extra = extra.astype(jnp.bfloat16)
    for k in range(spans):
        q_refs[k][rows:] = extra
    for copy in copies[1:]:
        copy.wait()


class Place:
    def __init__(self, spans, sizes, ways, counts_ref, mask_ref):
        self.spans, self.sizes, self.ways = spans, sizes, ways
        self.counts_ref, self.mask_ref = counts_ref, mask_ref
        self.me = lax.axis_index("span")
        self.at = [lax.axis_index(axis) for axis in ("ty", "tx")]

    def count(self, span, step_row=0, step_col=0):
        row, col = self.at[0] + step_row, self.at[1] + step_col
        return self.counts_ref[(span * self.sizes[0] + row) * self.sizes[1] + col]

    def bias(self, q_ref, span):
        slots = q_ref.shape[1] - EXTRA
        lanes = lax.broadcasted_iota(jnp.int32, (1, slots), 1)
        extra = q_ref[self.me ^ span, slots:, :HEAD_SIZE].astype(jnp.float32)
        parts = []
        for other in range(span + 1):
            opened = self.mask_ref[span * self.spans + other]
            for way in self.ways:
                if way is None:
                    chosen, near = extra[0:1], self.count(other)
                else:
                    dim, first = way
                    step = partner(self.at[dim], self.sizes[dim], first)
                    base = 1 + 2 * dim
                    chosen = jnp.where(step > 0, extra[base + 1 : base + 2], extra[base : base + 1])
                    near = self.count(other, *((step, 0) if dim == 0 else (0, step)))
                    near = jnp.where(step == 0, 0, near)
                near = jnp.where(opened > 0, near, 0)
                parts.append(jnp.where((lanes < near) & (chosen > 0), 0.0, DEAD))
        return jnp.concatenate(parts, axis=1)


def scores_of(q_ref, k, tile_refs, others, score_ref):
    tok_rows = q_ref.shape[1] - EXTRA
    groups = q_ref.shape[2] // HEAD_SIZE
    query = jnp.concatenate(
        [q_ref[k, :tok_rows, g * HEAD_SIZE : (g + 1) * HEAD_SIZE] for g in range(groups)], axis=0
    )
    keys = jnp.concatenate([t[other, 0] for other in others for t in tile_refs], axis=0)
    score_ref[:, : keys.shape[0]] = lax.dot_general(
        query, keys, (((1,), (1,)), ((), ())), preferred_element_type=jnp.float32
    )


def weigh(rows, bias, score_ref, weight_ref, before):
    blocks = range(bias.shape[1] // HEAD_SIZE)
    factor = HEAD_SIZE ** (-0.5) * math.log2(math.e)

    def block(b):
        lanes = slice(b * HEAD_SIZE, (b + 1) * HEAD_SIZE)
        return score_ref[rows, lanes] + bias[:, lanes]

    top = before
    for b in blocks:
        top = jnp.maximum(top, block(b))
    top = jnp.broadcast_to(jnp.max(top, axis=1, keepdims=True), top.shape)
    total = jnp.zeros(top.shape, jnp.float32)
    for b in blocks:
        weights = jnp.exp2((block(b) - top) * factor)
        total = total + weights
        weight_ref[rows, b * HEAD_SIZE : (b + 1) * HEAD_SIZE] = weights.astype(jnp.bfloat16)
    return top, total


def weighted(tile_refs, others, weight_ref):
    values = jnp.concatenate([t[other, 1] for other in others for t in tile_refs], axis=0)
    return jnp.dot(
        weight_ref[:, : values.shape[0]], values, preferred_element_type=jnp.float32
    )


def chunks(total):
    return [slice(start, start + CHUNK) for start in range(0, total, CHUNK)]


def attend_near(spans, sizes, ways, *refs):
    counts_ref, mask_ref, q_ref = refs[:3]
    tile_refs = refs[3 : 3 + len(ways)]
    top_ref, sum_ref, acc_ref, score_ref, weight_ref = refs[3 + len(ways) :]
    place = Place(spans, sizes, ways, counts_ref, mask_ref)
    for span in range(spans):
        others = [place.me ^ other for other in range(span + 1)]
        scores_of(q_ref, place.me ^ span, tile_refs, others, score_ref.at[span])
        bias = place.bias(q_ref, span)
        for rows in chunks(score_ref.shape[1]):
            before = jnp.full((CHUNK, HEAD_SIZE), DEAD, jnp.float32)
            top, total = weigh(rows, bias, score_ref.at[span], weight_ref.at[span], before)
            top_ref[span, rows] = top
            sum_ref[span, rows] = total
        acc_ref[span] = weighted(tile_refs, others, weight_ref.at[span])


def attend_far(spans, sizes, ways, k, *refs):
    counts_ref, mask_ref, q_ref = refs[:3]
    tile_refs = refs[3 : 3 + len(ways)]
    top_in, sum_in, acc_in, out_ref, score_ref, weight_ref, fade_ref, sum_ref = refs[3 + len(ways) :]
    place = Place(spans, sizes, ways, counts_ref, mask_ref)
    tok_rows = out_ref.shape[0]
    factor = HEAD_SIZE ** (-0.5) * math.log2(math.e)

    def finish(span, product):
        valid = place.count(span)
        for rows in chunks(acc_in.shape[1]):
            result = (acc_in[span, rows] * fade_ref[rows] + product[rows]) * sum_ref[rows]
            group, first = rows.start // tok_rows, rows.start % tok_rows
            ids = first + lax.broadcasted_iota(jnp.int32, (CHUNK, HEAD_SIZE), 0)
            out_ref[first : first + CHUNK, group * HEAD_SIZE : (group + 1) * HEAD_SIZE] = jnp.where(
                ids < valid, result, 0.0
            ).astype(jnp.bfloat16)

    for span in range(spans):

        @pl.when(place.me ^ k == span)
        def _(span=span):
            others = [place.me ^ other for other in range(span + 1)]
            scores_of(q_ref, k, tile_refs, others, score_ref)
            bias = place.bias(q_ref, span)
            for rows in chunks(score_ref.shape[0]):
                before = top_in[span, rows]
                top, total = weigh(rows, bias, score_ref, weight_ref, before)
                fade = jnp.exp2((before - top) * factor)
                total = jnp.sum(total + sum_in[span, rows] * fade, axis=1, keepdims=True)
                fade_ref[rows] = fade
                sum_ref[rows] = jnp.where(top > 0.5 * DEAD, 1.0 / total, jnp.nan)
            finish(span, weighted(tile_refs, others, weight_ref))


def join(spans, *refs):
    me = lax.axis_index("span")
    out_ref = refs[spans]
    width = refs[0].shape[1]
    for k in range(spans):
        start = pl.multiple_of((me ^ k) * width, HEAD_SIZE)
        out_ref[:, pl.ds(start, width)] = refs[k][...]


def shards(queries, key_value, pattern, counts, span_mask):
    spans, ty_count, tx_count = (lax.axis_size(a) for a in ("span", "ty", "tx"))
    tok_rows = queries.shape[3]
    kv_heads = key_value.shape[4] // (2 * HEAD_SIZE)
    assert kv_heads == spans and spans & (spans - 1) == 0
    width = queries.shape[4] // spans
    groups = width // HEAD_SIZE
    bf16 = jnp.bfloat16
    params = pltpu.CompilerParams(vmem_limit_bytes=VMEM_LIMIT)

    def exchange(block, k):
        return lax.ppermute(block, "span", [(i, i ^ k) for i in range(spans)])

    order = sorted(range(1, spans), key=lambda k: -bin(k).count("1"))

    pieces = pl.pallas_call(
        functools.partial(split, spans),
        out_shape=[jax.ShapeDtypeStruct((2, tok_rows, HEAD_SIZE), bf16)] * spans
        + [jax.ShapeDtypeStruct((tok_rows + EXTRA, width), bf16)] * spans,
        in_specs=[pl.BlockSpec(memory_space=pltpu.HBM)] * 3,
        out_specs=[vmem()] * (2 * spans),
        scratch_shapes=[
            pltpu.SMEM((NEIGH,), jnp.int32),
            pltpu.SemaphoreType.DMA((spans, 2)),
            pltpu.SemaphoreType.DMA((spans,)),
            pltpu.SemaphoreType.DMA,
        ],
        compiler_params=params,
        name="split",
    )(
        *(
            pltpu.with_memory_space_constraint(x, pltpu.HBM)
            for x in (
                pattern.reshape(NEIGH),
                key_value.reshape(tok_rows, -1),
                queries.reshape(tok_rows, -1),
            )
        )
    )
    kv_pieces, q_pieces = pieces[:spans], pieces[spans:]

    column = [kv_pieces[0]] + [None] * (spans - 1)
    for k in order:
        column[k] = exchange(kv_pieces[k], k)
    own = jnp.stack(column)
    q_here = [q_pieces[0]] + [None] * (spans - 1)
    for k in order:
        q_here[k] = exchange(q_pieces[k], k)

    near_ways, near, far_ways, far = [None], [own], [], []
    for first, pairs in enumerate(pairings(tx_count)):
        far_ways.append((1, first))
        far.append(swap(own, "tx", pairs))
    for first, pairs in enumerate(pairings(ty_count)):
        (near_ways if first == 0 else far_ways).append((0, first))
        (near if first == 0 else far).append(swap(own, "ty", pairs))

    sizes = (ty_count, tx_count)
    rows = groups * tok_rows
    q_all = jnp.stack(q_here)
    scalars = (counts.reshape(-1), span_mask.reshape(-1))
    states = pl.pallas_call(
        functools.partial(attend_near, spans, sizes, tuple(near_ways)),
        out_shape=[jax.ShapeDtypeStruct((spans, rows, HEAD_SIZE), jnp.float32)] * 3,
        in_specs=[smem(), smem()] + [vmem()] * (1 + len(near)),
        out_specs=[vmem()] * 3,
        scratch_shapes=[
            pltpu.VMEM((spans, rows, spans * len(near) * tok_rows), jnp.float32),
            pltpu.VMEM((spans, rows, spans * len(near) * tok_rows), bf16),
        ],
        compiler_params=params,
        cost_estimate=pl.CostEstimate(flops=NEAR_FLOPS, bytes_accessed=4_000_000, transcendentals=0),
        name="attend_near",
    )(*scalars, q_all, *near)
    outs = [None] * spans
    for k in order + [0]:
        outs[k] = pl.pallas_call(
            functools.partial(attend_far, spans, sizes, tuple(far_ways), k),
            out_shape=jax.ShapeDtypeStruct((tok_rows, width), bf16),
            in_specs=[smem(), smem()] + [vmem()] * (4 + len(far)),
            out_specs=vmem(),
            scratch_shapes=[
                pltpu.VMEM((rows, spans * len(far) * tok_rows), jnp.float32),
                pltpu.VMEM((rows, spans * len(far) * tok_rows), bf16),
                pltpu.VMEM((rows, HEAD_SIZE), jnp.float32),
                pltpu.VMEM((rows, HEAD_SIZE), jnp.float32),
            ],
            compiler_params=params,
            name=f"attend_far_{k}",
        )(*scalars, q_all, *far, *states)

    home = [outs[0]] + [None] * (spans - 1)
    for k in order:
        home[k] = exchange(outs[k], k)
    attended = pl.pallas_call(
        functools.partial(join, spans),
        out_shape=jax.ShapeDtypeStruct((tok_rows, spans * width), bf16),
        in_specs=[vmem()] * spans,
        out_specs=vmem(),
        compiler_params=params,
        name="join",
    )(*home)
    return attended.reshape(1, 1, 1, tok_rows, -1)


def solution(mesh):
    return jax.shard_map(
        shards,
        mesh=mesh,
        in_specs=(
            P("span", "ty", "tx", None, None),
            P("span", "ty", "tx", None, None),
            P("span", "ty", "tx", None),
            P(),
            P(),
        ),
        out_specs=P("span", "ty", "tx", None, None),
        check_vma=False,
    )
```

```python
import functools
import math

import jax
import jax.numpy as jnp
from jax import lax
from jax.experimental import pallas as pl
from jax.experimental.pallas import tpu as pltpu
from jax.sharding import PartitionSpec as P

HEAD_SIZE = 128
NEIGH = 5
EXTRA = 16
OWN_FLOPS = 10_000_000_000
LATER_FLOPS = 1_000_000
DEAD = -1e30
VMEM_LIMIT = 40 * 1024 * 1024


def vmem():
    return pl.BlockSpec(memory_space=pltpu.VMEM)


def smem():
    return pl.BlockSpec(memory_space=pltpu.SMEM)


def pairings(count):
    found = []
    for first in (0, 1):
        pairs = [(i, i + 1) for i in range(first, count - 1, 2)]
        if pairs:
            found.append(pairs)
    return found


def swap(block, sizes, dim, pairs):
    rows, cols = sizes
    paired = {i: j for a, b in pairs for i, j in ((a, b), (b, a))}
    moves = []
    for row in range(rows):
        for col in range(cols):
            place = [row, col]
            if place[dim] in paired:
                place[dim] = paired[place[dim]]
            elif dim == 1 and rows % 2 == 0:
                place[0] = row ^ 1
            else:
                continue
            moves.append((row * cols + col, place[0] * cols + place[1]))
    return lax.ppermute(block, ("ty", "tx"), moves)


def partner(place, count, first):
    low = lax.rem(place + first, 2) == 0
    step = jnp.where(low, 1, -1)
    other = place + step
    return jnp.where((other >= 0) & (other < count), step, 0)


def split(spans, pattern_hbm, kv_hbm, q_hbm, *refs):
    kv_refs, q_refs = refs[:spans], refs[spans : 2 * spans]
    pattern_ref, kv_sem, q_sem, pattern_sem = refs[2 * spans :]
    me = lax.axis_index("span")
    kv_width = kv_hbm.shape[1] // 2
    rows = q_hbm.shape[0]
    width = q_hbm.shape[1] // spans
    copies = [pltpu.make_async_copy(pattern_hbm, pattern_ref, pattern_sem)]
    for k in range(spans):
        head = me ^ k
        for part in range(2):
            start = pl.multiple_of(part * kv_width + head * HEAD_SIZE, HEAD_SIZE)
            copies.append(
                pltpu.make_async_copy(
                    kv_hbm.at[:, pl.ds(start, HEAD_SIZE)], kv_refs[k].at[part], kv_sem.at[k, part]
                )
            )
    for k in range(spans):
        start = pl.multiple_of((me ^ k) * width, HEAD_SIZE)
        copies.append(
            pltpu.make_async_copy(
                q_hbm.at[:, pl.ds(start, width)], q_refs[k].at[pl.ds(0, rows)], q_sem.at[k]
            )
        )
    for copy in copies:
        copy.start()
    copies[0].wait()
    row_ids = lax.broadcasted_iota(jnp.int32, (EXTRA, width), 0)
    extra = jnp.zeros((EXTRA, width), jnp.float32)
    for o in range(NEIGH):
        extra = jnp.where(row_ids == o, pattern_ref[o].astype(jnp.float32), extra)
    extra = extra.astype(jnp.bfloat16)
    for k in range(spans):
        q_refs[k][rows:] = extra
    for copy in copies[1:]:
        copy.wait()


def window_masks(spans, sizes, ways, counts_ref, mask_ref, q_ref, bias_ref, keep_ref):
    me = lax.axis_index("span")
    at = [lax.axis_index(axis) for axis in ("ty", "tx")]
    slots = q_ref.shape[1] - EXTRA
    lanes = lax.broadcasted_iota(jnp.int32, (1, slots), 1)
    row_ids = lax.broadcasted_iota(jnp.int32, (slots, HEAD_SIZE), 0)

    def count(span, step_row, step_col):
        return counts_ref[(span * sizes[0] + at[0] + step_row) * sizes[1] + at[1] + step_col]

    for span in range(spans):
        extra = q_ref[me ^ span, slots:, :HEAD_SIZE].astype(jnp.float32)
        keep_ref[span] = jnp.where(row_ids < count(span, 0, 0), 1.0, 0.0)
        for t, way in enumerate(ways):
            if way is None:
                chosen, move, here = extra[0:1], (0, 0), True
            else:
                dim, first = way
                step = partner(at[dim], sizes[dim], first)
                base = 1 + 2 * dim
                chosen = jnp.where(step > 0, extra[base + 1 : base + 2], extra[base : base + 1])
                move, here = ((step, 0) if dim == 0 else (0, step)), step != 0
            for other in range(span + 1):
                seen = (mask_ref[span * spans + other] > 0) & here
                near = jnp.where(seen, count(other, *move), 0)
                bias_ref[span, t : t + 1, other * slots : (other + 1) * slots] = jnp.where(
                    (lanes < near) & (chosen > 0), 0.0, DEAD
                )


def attend(spans, sizes, ways, number, *refs):
    first, last = number == 0, number == len(ways) - 1
    if first:
        (counts_ref, mask_ref, q_ref, tile_ref), refs = refs[:4], refs[4:]
    else:
        (q_ref, tile_ref, bias_ref, keep_ref, top_in, sum_in, acc_in), refs = refs[:7], refs[7:]
    if last:
        (out_ref,), refs = refs[:1], refs[1:]
    else:
        (top_ref, sum_ref, acc_ref), refs = refs[:3], refs[3:]
    if first:
        (bias_ref, keep_ref), refs = refs[:2], refs[2:]
        window_masks(spans, sizes, ways, counts_ref, mask_ref, q_ref, bias_ref, keep_ref)
    (score_ref,) = refs
    me = lax.axis_index("span")
    tok_rows = q_ref.shape[1] - EXTRA
    groups = q_ref.shape[2] // HEAD_SIZE
    factor = HEAD_SIZE ** (-0.5) * math.log2(math.e)

    def gathered(span, part):
        return jnp.concatenate([tile_ref[me ^ other, part] for other in range(span + 1)], axis=0)

    def score(span):
        query = jnp.concatenate(
            [q_ref[me ^ span, :tok_rows, g * HEAD_SIZE : (g + 1) * HEAD_SIZE] for g in range(groups)],
            axis=0,
        )
        keys = gathered(span, 0)
        score_ref[span, :, : keys.shape[0]] = lax.dot_general(
            query, keys, (((1,), (1,)), ((), ())), preferred_element_type=jnp.float32
        )

    def weigh(span):
        values = gathered(span, 1)
        bias = bias_ref[span, number : number + 1, : values.shape[0]]
        blocks = [slice(b, b + HEAD_SIZE) for b in range(0, values.shape[0], HEAD_SIZE)]
        for g in range(groups):
            rows = slice(g * tok_rows, (g + 1) * tok_rows)
            shape = (tok_rows, HEAD_SIZE)
            before = jnp.full(shape, DEAD, jnp.float32) if first else top_in[span, rows]
            top = before
            for lanes in blocks:
                top = jnp.maximum(top, score_ref[span, rows, lanes] + bias[:, lanes])
            top = jnp.broadcast_to(jnp.max(top, axis=1, keepdims=True), shape)
            total, weights = jnp.zeros(shape, jnp.float32), []
            for lanes in blocks:
                weight = jnp.exp2((score_ref[span, rows, lanes] + bias[:, lanes] - top) * factor)
                total = total + weight
                weights.append(weight.astype(jnp.bfloat16))
            result = jnp.dot(
                jnp.concatenate(weights, axis=1), values, preferred_element_type=jnp.float32
            )
            if not first:
                fade = jnp.exp2((before - top) * factor)
                total = total + sum_in[span, rows] * fade
                result = result + acc_in[span, rows] * fade
            if not last:
                top_ref[span, rows], sum_ref[span, rows], acc_ref[span, rows] = top, total, result
                continue
            share = 1.0 / jnp.sum(total, axis=1, keepdims=True)
            result = result * jnp.where(top > 0.5 * DEAD, share, jnp.nan)
            out_ref[me ^ span, :, g * HEAD_SIZE : (g + 1) * HEAD_SIZE] = jnp.where(
                keep_ref[span] > 0, result, 0.0
            ).astype(jnp.bfloat16)

    score(0)
    for span in range(spans):
        if span + 1 < spans:
            score(span + 1)
        weigh(span)


def join(spans, *refs):
    me = lax.axis_index("span")
    out_ref = refs[spans]
    width = refs[0].shape[1]
    for k in range(spans):
        start = pl.multiple_of((me ^ k) * width, HEAD_SIZE)
        out_ref[:, pl.ds(start, width)] = refs[k][...]


def shards(queries, key_value, pattern, counts, span_mask):
    spans, ty_count, tx_count = (lax.axis_size(a) for a in ("span", "ty", "tx"))
    tok_rows = queries.shape[3]
    kv_heads = key_value.shape[4] // (2 * HEAD_SIZE)
    assert kv_heads == spans and spans & (spans - 1) == 0
    width = queries.shape[4] // spans
    groups = width // HEAD_SIZE
    bf16 = jnp.bfloat16
    params = pltpu.CompilerParams(vmem_limit_bytes=VMEM_LIMIT)

    def exchange(block, k):
        return lax.ppermute(block, "span", [(i, i ^ k) for i in range(spans)])

    sizes = (ty_count, tx_count)
    order = sorted(range(1, spans), key=lambda k: -bin(k).count("1"))

    pieces = pl.pallas_call(
        functools.partial(split, spans),
        out_shape=[jax.ShapeDtypeStruct((2, tok_rows, HEAD_SIZE), bf16)] * spans
        + [jax.ShapeDtypeStruct((tok_rows + EXTRA, width), bf16)] * spans,
        in_specs=[pl.BlockSpec(memory_space=pltpu.HBM)] * 3,
        out_specs=[vmem()] * (2 * spans),
        scratch_shapes=[
            pltpu.SMEM((NEIGH,), jnp.int32),
            pltpu.SemaphoreType.DMA((spans, 2)),
            pltpu.SemaphoreType.DMA((spans,)),
            pltpu.SemaphoreType.DMA,
        ],
        compiler_params=params,
        name="split",
    )(
        *(
            pltpu.with_memory_space_constraint(x, pltpu.HBM)
            for x in (
                pattern.reshape(NEIGH),
                key_value.reshape(tok_rows, -1),
                queries.reshape(tok_rows, -1),
            )
        )
    )
    kv_pieces, q_pieces = pieces[:spans], pieces[spans:]

    column = [kv_pieces[0]] + [None] * (spans - 1)
    for k in order:
        column[k] = exchange(kv_pieces[k], k)
    own = jnp.stack(column)
    q_here = [q_pieces[0]] + [None] * (spans - 1)
    for k in order:
        q_here[k] = exchange(q_pieces[k], k)

    sizes = (ty_count, tx_count)
    rows = groups * tok_rows
    q_all = jnp.stack(q_here)
    scalars = (counts.reshape(-1), span_mask.reshape(-1))

    ways, tiles = [None], [own]
    for dim, backwards in ((0, False), (1, True)):
        found = list(enumerate(pairings(sizes[dim])))
        for first, pairs in reversed(found) if backwards else found:
            ways.append((dim, first))
            tiles.append(swap(own, sizes, dim, pairs))

    kept = jax.ShapeDtypeStruct((spans, rows, HEAD_SIZE), jnp.float32)
    bias = jax.ShapeDtypeStruct((spans, 8, spans * tok_rows), jnp.float32)
    keep = jax.ShapeDtypeStruct((spans, tok_rows, HEAD_SIZE), jnp.float32)
    result = jax.ShapeDtypeStruct((spans, tok_rows, width), bf16)
    masks = state = ()
    for number, tile in enumerate(tiles):
        first, last = number == 0, number == len(tiles) - 1
        outs = ([result] if last else [kept] * 3) + ([bias, keep] if first else [])
        given = (*scalars, q_all, tile) if first else (q_all, tile, *masks, *state)
        state = pl.pallas_call(
            functools.partial(attend, spans, sizes, tuple(ways), number),
            out_shape=outs,
            in_specs=([smem()] * 2 + [vmem()] * 2) if first else [vmem()] * len(given),
            out_specs=[vmem()] * len(outs),
            scratch_shapes=[pltpu.VMEM((spans, rows, spans * tok_rows), jnp.float32)],
            compiler_params=params,
            cost_estimate=pl.CostEstimate(
                flops=OWN_FLOPS if first else LATER_FLOPS, bytes_accessed=4_000_000, transcendentals=0
            ),
            name=f"attend_{number}",
        )(*given)
        if first and not last:
            state, masks = state[:3], state[3:]
    outs = state[0]

    home = [outs[0]] + [None] * (spans - 1)
    for k in order:
        home[k] = exchange(outs[k], k)
    attended = pl.pallas_call(
        functools.partial(join, spans),
        out_shape=jax.ShapeDtypeStruct((tok_rows, spans * width), bf16),
        in_specs=[vmem()] * spans,
        out_specs=vmem(),
        compiler_params=params,
        name="join",
    )(*home)
    return attended.reshape(1, 1, 1, tok_rows, -1)


def solution(mesh):
    return jax.shard_map(
        shards,
        mesh=mesh,
        in_specs=(
            P("span", "ty", "tx", None, None),
            P("span", "ty", "tx", None, None),
            P("span", "ty", "tx", None),
            P(),
            P(),
        ),
        out_specs=P("span", "ty", "tx", None, None),
        check_vma=False,
    )
```

```python
import functools
import math

import jax
import jax.numpy as jnp
from jax import lax
from jax.experimental import pallas as pl
from jax.experimental.pallas import tpu as pltpu
from jax.sharding import PartitionSpec as P

HEAD_SIZE = 128
NEIGH = 5
EXTRA = 16
OWN_FLOPS = 10_000_000_000
LATER_FLOPS = 1_000_000
DEAD = -1e30
VMEM_LIMIT = 40 * 1024 * 1024


def vmem():
    return pl.BlockSpec(memory_space=pltpu.VMEM)


def smem():
    return pl.BlockSpec(memory_space=pltpu.SMEM)


def pairings(count):
    found = []
    for first in (0, 1):
        pairs = [(i, i + 1) for i in range(first, count - 1, 2)]
        if pairs:
            found.append(pairs)
    return found


def swap(block, sizes, dim, pairs):
    rows, cols = sizes
    paired = {i: j for a, b in pairs for i, j in ((a, b), (b, a))}
    moves = []
    for row in range(rows):
        for col in range(cols):
            place = [row, col]
            if place[dim] in paired:
                place[dim] = paired[place[dim]]
            elif dim == 1 and rows % 2 == 0:
                place[0] = row ^ 1
            else:
                continue
            moves.append((row * cols + col, place[0] * cols + place[1]))
    return lax.ppermute(block, ("ty", "tx"), moves)


def partner(place, count, first):
    low = lax.rem(place + first, 2) == 0
    step = jnp.where(low, 1, -1)
    other = place + step
    return jnp.where((other >= 0) & (other < count), step, 0)


def split(spans, pattern_hbm, kv_hbm, q_hbm, *refs):
    kv_refs, q_refs = refs[:spans], refs[spans : 2 * spans]
    pattern_ref, kv_sem, q_sem, pattern_sem = refs[2 * spans :]
    me = lax.axis_index("span")
    kv_width = kv_hbm.shape[1] // 2
    rows = q_hbm.shape[0]
    width = q_hbm.shape[1] // spans
    copies = [pltpu.make_async_copy(pattern_hbm, pattern_ref, pattern_sem)]
    for k in range(spans):
        head = me ^ k
        for part in range(2):
            start = pl.multiple_of(part * kv_width + head * HEAD_SIZE, HEAD_SIZE)
            copies.append(
                pltpu.make_async_copy(
                    kv_hbm.at[:, pl.ds(start, HEAD_SIZE)], kv_refs[k].at[part], kv_sem.at[k, part]
                )
            )
    for k in range(spans):
        start = pl.multiple_of((me ^ k) * width, HEAD_SIZE)
        copies.append(
            pltpu.make_async_copy(
                q_hbm.at[:, pl.ds(start, width)], q_refs[k].at[pl.ds(0, rows)], q_sem.at[k]
            )
        )
    for copy in copies:
        copy.start()
    copies[0].wait()
    row_ids = lax.broadcasted_iota(jnp.int32, (EXTRA, width), 0)
    extra = jnp.zeros((EXTRA, width), jnp.float32)
    for o in range(NEIGH):
        extra = jnp.where(row_ids == o, pattern_ref[o].astype(jnp.float32), extra)
    extra = extra.astype(jnp.bfloat16)
    for k in range(spans):
        q_refs[k][rows:] = extra
    for copy in copies[1:]:
        copy.wait()


def window_masks(spans, sizes, ways, counts_ref, mask_ref, q_ref, bias_ref, keep_ref):
    me = lax.axis_index("span")
    at = [lax.axis_index(axis) for axis in ("ty", "tx")]
    slots = q_ref.shape[1] - EXTRA
    lanes = lax.broadcasted_iota(jnp.int32, (1, slots), 1)
    row_ids = lax.broadcasted_iota(jnp.int32, (slots, HEAD_SIZE), 0)

    def count(span, step_row, step_col):
        return counts_ref[(span * sizes[0] + at[0] + step_row) * sizes[1] + at[1] + step_col]

    for span in range(spans):
        extra = q_ref[me ^ span, slots:, :HEAD_SIZE].astype(jnp.float32)
        keep_ref[span] = jnp.where(row_ids < count(span, 0, 0), 1.0, 0.0)
        for t, way in enumerate(ways):
            if way is None:
                chosen, move, here = extra[0:1], (0, 0), True
            else:
                dim, first = way
                step = partner(at[dim], sizes[dim], first)
                base = 1 + 2 * dim
                chosen = jnp.where(step > 0, extra[base + 1 : base + 2], extra[base : base + 1])
                move, here = ((step, 0) if dim == 0 else (0, step)), step != 0
            for other in range(span + 1):
                seen = (mask_ref[span * spans + other] > 0) & here
                near = jnp.where(seen, count(other, *move), 0)
                bias_ref[span, t : t + 1, other * slots : (other + 1) * slots] = jnp.where(
                    (lanes < near) & (chosen > 0), 0.0, DEAD
                )


def attend(spans, sizes, ways, number, *refs):
    first, last = number == 0, number == len(ways) - 1
    if first:
        (counts_ref, mask_ref, q_ref, tile_ref), refs = refs[:4], refs[4:]
    else:
        (q_ref, tile_ref, bias_ref, keep_ref, top_in, sum_in, acc_in), refs = refs[:7], refs[7:]
    if last:
        (out_ref,), refs = refs[:1], refs[1:]
    else:
        (top_ref, sum_ref, acc_ref), refs = refs[:3], refs[3:]
    if first:
        (bias_ref, keep_ref), refs = refs[:2], refs[2:]
        window_masks(spans, sizes, ways, counts_ref, mask_ref, q_ref, bias_ref, keep_ref)
    (score_ref,) = refs
    me = lax.axis_index("span")
    tok_rows = q_ref.shape[1] - EXTRA
    groups = q_ref.shape[2] // HEAD_SIZE
    factor = HEAD_SIZE ** (-0.5) * math.log2(math.e)

    def gathered(span, part):
        return jnp.concatenate([tile_ref[me ^ other, part] for other in range(span + 1)], axis=0)

    def score(span):
        query = jnp.concatenate(
            [q_ref[me ^ span, :tok_rows, g * HEAD_SIZE : (g + 1) * HEAD_SIZE] for g in range(groups)],
            axis=0,
        )
        keys = gathered(span, 0)
        score_ref[span, :, : keys.shape[0]] = lax.dot_general(
            query, keys, (((1,), (1,)), ((), ())), preferred_element_type=jnp.float32
        )

    def weigh(span):
        values = gathered(span, 1)
        bias = bias_ref[span, number : number + 1, : values.shape[0]]
        blocks = [slice(b, b + HEAD_SIZE) for b in range(0, values.shape[0], HEAD_SIZE)]
        for g in range(groups):
            rows = slice(g * tok_rows, (g + 1) * tok_rows)
            shape = (tok_rows, HEAD_SIZE)
            before = jnp.full(shape, DEAD, jnp.float32) if first else top_in[span, rows]
            top = before
            for lanes in blocks:
                top = jnp.maximum(top, score_ref[span, rows, lanes] + bias[:, lanes])
            top = jnp.broadcast_to(jnp.max(top, axis=1, keepdims=True), shape)
            total, weights = jnp.zeros(shape, jnp.float32), []
            for lanes in blocks:
                weight = jnp.exp2((score_ref[span, rows, lanes] + bias[:, lanes] - top) * factor)
                total = total + weight
                weights.append(weight.astype(jnp.bfloat16))
            result = jnp.dot(
                jnp.concatenate(weights, axis=1), values, preferred_element_type=jnp.float32
            )
            if not first:
                fade = jnp.exp2((before - top) * factor)
                total = total + sum_in[span, rows] * fade
                result = result + acc_in[span, rows] * fade
            if not last:
                top_ref[span, rows], sum_ref[span, rows], acc_ref[span, rows] = top, total, result
                continue
            share = 1.0 / jnp.sum(total, axis=1, keepdims=True)
            result = result * jnp.where(top > 0.5 * DEAD, share, jnp.nan)
            out_ref[me ^ span, :, g * HEAD_SIZE : (g + 1) * HEAD_SIZE] = jnp.where(
                keep_ref[span] > 0, result, 0.0
            ).astype(jnp.bfloat16)

    score(0)
    for span in range(spans):
        if span + 1 < spans:
            score(span + 1)
        weigh(span)


def collect(spans, own_ref, *refs):
    q_refs, (q_all_ref, copy_ref) = refs[:spans], refs[spans:]
    for k in range(spans):
        q_all_ref[k] = q_refs[k][...]
    copy_ref[...] = own_ref[...]


def join(spans, *refs):
    me = lax.axis_index("span")
    out_ref = refs[spans]
    width = refs[0].shape[1]
    for k in range(spans):
        start = pl.multiple_of((me ^ k) * width, HEAD_SIZE)
        out_ref[:, pl.ds(start, width)] = refs[k][...]


def shards(queries, key_value, pattern, counts, span_mask):
    spans, ty_count, tx_count = (lax.axis_size(a) for a in ("span", "ty", "tx"))
    tok_rows = queries.shape[3]
    kv_heads = key_value.shape[4] // (2 * HEAD_SIZE)
    assert kv_heads == spans and spans & (spans - 1) == 0
    width = queries.shape[4] // spans
    groups = width // HEAD_SIZE
    bf16 = jnp.bfloat16
    params = pltpu.CompilerParams(vmem_limit_bytes=VMEM_LIMIT)

    def exchange(block, k):
        return lax.ppermute(block, "span", [(i, i ^ k) for i in range(spans)])

    sizes = (ty_count, tx_count)
    order = sorted(range(1, spans), key=lambda k: -bin(k).count("1"))

    pieces = pl.pallas_call(
        functools.partial(split, spans),
        out_shape=[jax.ShapeDtypeStruct((2, tok_rows, HEAD_SIZE), bf16)] * spans
        + [jax.ShapeDtypeStruct((tok_rows + EXTRA, width), bf16)] * spans,
        in_specs=[pl.BlockSpec(memory_space=pltpu.HBM)] * 3,
        out_specs=[vmem()] * (2 * spans),
        scratch_shapes=[
            pltpu.SMEM((NEIGH,), jnp.int32),
            pltpu.SemaphoreType.DMA((spans, 2)),
            pltpu.SemaphoreType.DMA((spans,)),
            pltpu.SemaphoreType.DMA,
        ],
        compiler_params=params,
        name="split",
    )(
        *(
            pltpu.with_memory_space_constraint(x, pltpu.HBM)
            for x in (
                pattern.reshape(NEIGH),
                key_value.reshape(tok_rows, -1),
                queries.reshape(tok_rows, -1),
            )
        )
    )
    kv_pieces, q_pieces = pieces[:spans], pieces[spans:]

    column = [kv_pieces[0]] + [None] * (spans - 1)
    for k in order:
        column[k] = exchange(kv_pieces[k], k)
    own = jnp.stack(column)
    q_here = [q_pieces[0]] + [None] * (spans - 1)
    for k in order:
        q_here[k] = exchange(q_pieces[k], k)

    sizes = (ty_count, tx_count)
    rows = groups * tok_rows
    q_all, own_copy = pl.pallas_call(
        functools.partial(collect, spans),
        out_shape=[
            jax.ShapeDtypeStruct((spans, *q_here[0].shape), bf16),
            jax.ShapeDtypeStruct(own.shape, bf16),
        ],
        in_specs=[vmem()] * (1 + spans),
        out_specs=[vmem()] * 2,
        compiler_params=params,
        name="collect",
    )(own, *q_here)
    scalars = (counts.reshape(-1), span_mask.reshape(-1))

    ways, tiles = [None], [own]
    for dim, backwards in ((0, False), (1, False)):
        found = list(enumerate(pairings(sizes[dim])))
        for first, pairs in reversed(found) if backwards else found:
            ways.append((dim, first))
            tiles.append(swap(own if dim else own_copy, sizes, dim, pairs))

    kept = jax.ShapeDtypeStruct((spans, rows, HEAD_SIZE), jnp.float32)
    bias = jax.ShapeDtypeStruct((spans, 8, spans * tok_rows), jnp.float32)
    keep = jax.ShapeDtypeStruct((spans, tok_rows, HEAD_SIZE), jnp.float32)
    result = jax.ShapeDtypeStruct((spans, tok_rows, width), bf16)
    masks = state = ()
    for number, tile in enumerate(tiles):
        first, last = number == 0, number == len(tiles) - 1
        outs = ([result] if last else [kept] * 3) + ([bias, keep] if first else [])
        given = (*scalars, q_all, tile) if first else (q_all, tile, *masks, *state)
        state = pl.pallas_call(
            functools.partial(attend, spans, sizes, tuple(ways), number),
            out_shape=outs,
            in_specs=([smem()] * 2 + [vmem()] * 2) if first else [vmem()] * len(given),
            out_specs=[vmem()] * len(outs),
            scratch_shapes=[pltpu.VMEM((spans, rows, spans * tok_rows), jnp.float32)],
            compiler_params=params,
            cost_estimate=pl.CostEstimate(
                flops=OWN_FLOPS if first else LATER_FLOPS, bytes_accessed=4_000_000, transcendentals=0
            ),
            name=f"attend_{number}",
        )(*given)
        if first and not last:
            state, masks = state[:3], state[3:]
    outs = state[0]

    home = [outs[0]] + [None] * (spans - 1)
    for k in order:
        home[k] = exchange(outs[k], k)
    attended = pl.pallas_call(
        functools.partial(join, spans),
        out_shape=jax.ShapeDtypeStruct((tok_rows, spans * width), bf16),
        in_specs=[vmem()] * spans,
        out_specs=vmem(),
        compiler_params=params,
        name="join",
    )(*home)
    return attended.reshape(1, 1, 1, tok_rows, -1)


def solution(mesh):
    return jax.shard_map(
        shards,
        mesh=mesh,
        in_specs=(
            P("span", "ty", "tx", None, None),
            P("span", "ty", "tx", None, None),
            P("span", "ty", "tx", None),
            P(),
            P(),
        ),
        out_specs=P("span", "ty", "tx", None, None),
        check_vma=False,
    )
```

```python
import functools
import math

import jax
import jax.numpy as jnp
from jax import lax
from jax.experimental import pallas as pl
from jax.experimental.pallas import tpu as pltpu
from jax.sharding import PartitionSpec as P

HEAD_SIZE = 128
NEIGH = 5
EXTRA = 16
OWN_FLOPS = 10_000_000_000
LATER_FLOPS = 1_000_000
CUTS = (1, 2)
SMALL = pl.CostEstimate(flops=1000, bytes_accessed=1000, transcendentals=0)
DEAD = -1e30
VMEM_LIMIT = 40 * 1024 * 1024


def vmem():
    return pl.BlockSpec(memory_space=pltpu.VMEM)


def smem():
    return pl.BlockSpec(memory_space=pltpu.SMEM)


def pairings(count):
    found = []
    for first in (0, 1):
        pairs = [(i, i + 1) for i in range(first, count - 1, 2)]
        if pairs:
            found.append(pairs)
    return found


def swap(block, sizes, dim, pairs):
    rows, cols = sizes
    paired = {i: j for a, b in pairs for i, j in ((a, b), (b, a))}
    moves = []
    for row in range(rows):
        for col in range(cols):
            place = [row, col]
            if place[dim] in paired:
                place[dim] = paired[place[dim]]
            elif dim == 1 and rows % 2 == 0:
                place[0] = row ^ 1
            else:
                continue
            moves.append((row * cols + col, place[0] * cols + place[1]))
    return lax.ppermute(block, ("ty", "tx"), moves)


def partner(place, count, first):
    low = lax.rem(place + first, 2) == 0
    step = jnp.where(low, 1, -1)
    other = place + step
    return jnp.where((other >= 0) & (other < count), step, 0)


def split(spans, sizes, ways, *refs):
    (pattern_hbm, counts_hbm, mask_hbm, kv_hbm, q_hbm), refs = refs[:5], refs[5:]
    kv_refs, q_refs, refs = refs[:spans], refs[spans : 2 * spans], refs[2 * spans :]
    bias_ref, keep_ref, pattern_ref, counts_ref, mask_ref, kv_ref, q_ref, sems = refs
    me = lax.axis_index("span")
    at = [lax.axis_index(axis) for axis in ("ty", "tx")]
    kv_width = kv_hbm.shape[1] // 2
    rows = q_hbm.shape[0]
    width = q_hbm.shape[1] // spans
    copies = [
        pltpu.make_async_copy(source, target, sems.at[i])
        for i, (source, target) in enumerate(
            (
                (pattern_hbm, pattern_ref),
                (counts_hbm, counts_ref),
                (mask_hbm, mask_ref),
                (kv_hbm, kv_ref),
                (q_hbm, q_ref),
            )
        )
    ]
    for copy in copies:
        copy.start()
    for copy in copies[:3]:
        copy.wait()
    row_ids = lax.broadcasted_iota(jnp.int32, (EXTRA, width), 0)
    extra = jnp.zeros((EXTRA, width), jnp.float32)
    for o in range(NEIGH):
        extra = jnp.where(row_ids == o, pattern_ref[o].astype(jnp.float32), extra)
    extra = extra.astype(jnp.bfloat16)
    for k in range(spans):
        q_refs[k][rows:] = extra

    lanes = lax.broadcasted_iota(jnp.int32, (1, rows), 1)
    row_ids = lax.broadcasted_iota(jnp.int32, (rows, HEAD_SIZE), 0)

    def count(span, step_row, step_col):
        return counts_ref[span, at[0] + step_row, at[1] + step_col]

    for other in range(spans):
        keep_ref[other] = jnp.where(row_ids < count(other, 0, 0), 1.0, 0.0)
        for t, way in enumerate(ways):
            if way is None:
                near = count(other, 0, 0)
            else:
                step = partner(at[way[0]], sizes[way[0]], way[1])
                near = count(other, *((step, 0) if way[0] == 0 else (0, step)))
                near = jnp.where(step == 0, 0, near)
            for span in range(other, spans):
                seen = jnp.where(mask_ref[span, other] > 0, near, 0)
                bias_ref[span, t : t + 1, other * rows : (other + 1) * rows] = jnp.where(
                    lanes < seen, 0.0, DEAD
                )

    copies[3].wait()
    for k in range(spans):
        for part in range(2):
            start = pl.multiple_of(part * kv_width + (me ^ k) * HEAD_SIZE, HEAD_SIZE)
            kv_refs[k][part] = kv_ref[:, pl.ds(start, HEAD_SIZE)]
    copies[4].wait()
    for k in range(spans):
        q_refs[k][:rows] = q_ref[:, pl.ds(pl.multiple_of((me ^ k) * width, HEAD_SIZE), width)]


def attend(spans, sizes, ways, numbers, *refs):
    first, last = numbers[0] == 0, numbers[-1] == len(ways) - 1
    q_ref, refs = refs[0], refs[1:]
    tile_refs, refs = refs[: len(numbers)], refs[len(numbers) :]
    (bias_ref, keep_ref), refs = refs[:2], refs[2:]
    if not first:
        (top_in, sum_in, acc_in), refs = refs[:3], refs[3:]
    if last:
        (out_ref,), refs = refs[:1], refs[1:]
    else:
        (top_ref, sum_ref, acc_ref), refs = refs[:3], refs[3:]
    (score_ref,) = refs
    me = lax.axis_index("span")
    tok_rows = q_ref.shape[1] - EXTRA
    groups = q_ref.shape[2] // HEAD_SIZE
    factor = HEAD_SIZE ** (-0.5) * math.log2(math.e)

    def pattern_rows(n):
        if ways[n] is None:
            return 0, 0
        base = 1 + 2 * ways[n][0]
        return base, base + 1

    steps = [
        None
        if ways[n] is None
        else partner(lax.axis_index(("ty", "tx")[ways[n][0]]), sizes[ways[n][0]], ways[n][1])
        for n in numbers
    ]

    def bias_of(span):
        extra = q_ref[me ^ span, tok_rows:, :HEAD_SIZE].astype(jnp.float32)
        parts = []
        for n, step in zip(numbers, steps, strict=True):
            low, high = pattern_rows(n)
            chosen = extra[low : low + 1]
            if step is not None:
                chosen = jnp.where(step > 0, extra[high : high + 1], chosen)
            closed = jnp.where(chosen > 0, 0.0, DEAD)
            for other in range(span + 1):
                lanes = slice(other * tok_rows, (other + 1) * tok_rows)
                parts.append(bias_ref[span, n : n + 1, lanes] + closed)
        return jnp.concatenate(parts, axis=1)

    def gathered(span, part):
        return jnp.concatenate([t[me ^ o, part] for t in tile_refs for o in range(span + 1)], axis=0)

    def score(span):
        query = jnp.concatenate(
            [q_ref[me ^ span, :tok_rows, g * HEAD_SIZE : (g + 1) * HEAD_SIZE] for g in range(groups)],
            axis=0,
        )
        keys = gathered(span, 0)
        score_ref[span, :, : keys.shape[0]] = lax.dot_general(
            query, keys, (((1,), (1,)), ((), ())), preferred_element_type=jnp.float32
        )

    def weigh(span):
        values = gathered(span, 1)
        bias = bias_of(span)
        blocks = [slice(b, b + HEAD_SIZE) for b in range(0, values.shape[0], HEAD_SIZE)]
        for g in range(groups):
            rows = slice(g * tok_rows, (g + 1) * tok_rows)
            shape = (tok_rows, HEAD_SIZE)
            before = jnp.full(shape, DEAD, jnp.float32) if first else top_in[span, rows]
            top = before
            for lanes in blocks:
                top = jnp.maximum(top, score_ref[span, rows, lanes] + bias[:, lanes])
            top = jnp.broadcast_to(jnp.max(top, axis=1, keepdims=True), shape)
            total, weights = jnp.zeros(shape, jnp.float32), []
            for lanes in blocks:
                weight = jnp.exp2((score_ref[span, rows, lanes] + bias[:, lanes] - top) * factor)
                total = total + weight
                weights.append(weight.astype(jnp.bfloat16))
            result = jnp.dot(
                jnp.concatenate(weights, axis=1), values, preferred_element_type=jnp.float32
            )
            if not first:
                fade = jnp.exp2((before - top) * factor)
                total = total + sum_in[span, rows] * fade
                result = result + acc_in[span, rows] * fade
            if not last:
                top_ref[span, rows], sum_ref[span, rows], acc_ref[span, rows] = top, total, result
                continue
            share = 1.0 / jnp.sum(total, axis=1, keepdims=True)
            result = result * jnp.where(top > 0.5 * DEAD, share, jnp.nan)
            out_ref[me ^ span, :, g * HEAD_SIZE : (g + 1) * HEAD_SIZE] = jnp.where(
                keep_ref[span] > 0, result, 0.0
            ).astype(jnp.bfloat16)

    score(0)
    for span in range(spans):
        if span + 1 < spans:
            score(span + 1)
        weigh(span)


def collect(spans, own_ref, *refs):
    q_refs, (q_all_ref, copy_ref) = refs[:spans], refs[spans:]
    for k in range(spans):
        q_all_ref[k] = q_refs[k][...]
    copy_ref[...] = own_ref[...]


def join(places, *refs):
    me = lax.axis_index("span")
    out_ref = refs[-1]
    for k, ref in zip(places, refs, strict=False):
        width = ref.shape[1]
        start = pl.multiple_of((me ^ k) * width, HEAD_SIZE)
        out_ref[:, pl.ds(start, width)] = ref[...]


def shards(queries, key_value, pattern, counts, span_mask):
    spans, ty_count, tx_count = (lax.axis_size(a) for a in ("span", "ty", "tx"))
    tok_rows = queries.shape[3]
    kv_heads = key_value.shape[4] // (2 * HEAD_SIZE)
    assert kv_heads == spans and spans & (spans - 1) == 0
    width = queries.shape[4] // spans
    groups = width // HEAD_SIZE
    bf16 = jnp.bfloat16
    params = pltpu.CompilerParams(vmem_limit_bytes=VMEM_LIMIT)

    def exchange(block, k):
        return lax.ppermute(block, "span", [(i, i ^ k) for i in range(spans)])

    sizes = (ty_count, tx_count)
    order = sorted(range(1, spans), key=lambda k: -bin(k).count("1"))

    swaps = [
        (dim, first, pairs) for dim in (0, 1) for first, pairs in enumerate(pairings(sizes[dim]))
    ]
    ways = (None, *((dim, first) for dim, first, _ in swaps))
    piece = jax.ShapeDtypeStruct((2, tok_rows, HEAD_SIZE), bf16)
    pieces = pl.pallas_call(
        functools.partial(split, spans, sizes, ways),
        out_shape=[piece] * spans
        + [jax.ShapeDtypeStruct((tok_rows + EXTRA, width), bf16)] * spans
        + [
            jax.ShapeDtypeStruct((spans, 8, spans * tok_rows), jnp.float32),
            jax.ShapeDtypeStruct((spans, tok_rows, HEAD_SIZE), jnp.float32),
        ],
        in_specs=[pl.BlockSpec(memory_space=pltpu.HBM)] * 5,
        out_specs=[vmem()] * (2 * spans + 2),
        scratch_shapes=[
            pltpu.SMEM((NEIGH,), jnp.int32),
            pltpu.SMEM(counts.shape, jnp.int32),
            pltpu.SMEM(span_mask.shape, jnp.int32),
            pltpu.VMEM((tok_rows, 2 * kv_heads * HEAD_SIZE), bf16),
            pltpu.VMEM((tok_rows, spans * width), bf16),
            pltpu.SemaphoreType.DMA((5,)),
        ],
        compiler_params=params,
        name="split",
    )(
        *(
            pltpu.with_memory_space_constraint(x, pltpu.HBM)
            for x in (
                pattern.reshape(NEIGH),
                counts,
                span_mask,
                key_value.reshape(tok_rows, -1),
                queries.reshape(tok_rows, -1),
            )
        )
    )
    kv_pieces, q_pieces, masks = pieces[:spans], pieces[spans : 2 * spans], pieces[2 * spans :]

    column = [kv_pieces[0]] + [None] * (spans - 1)
    for k in order:
        column[k] = exchange(kv_pieces[k], k)
    own = jnp.stack(column)
    q_here = [q_pieces[0]] + [None] * (spans - 1)
    for k in order:
        q_here[k] = exchange(q_pieces[k], k)

    sizes = (ty_count, tx_count)
    rows = groups * tok_rows
    q_all, own_copy = pl.pallas_call(
        functools.partial(collect, spans),
        out_shape=[
            jax.ShapeDtypeStruct((spans, *q_here[0].shape), bf16),
            jax.ShapeDtypeStruct(own.shape, bf16),
        ],
        in_specs=[vmem()] * (1 + spans),
        out_specs=[vmem()] * 2,
        compiler_params=params,
        name="collect",
    )(own, *q_here)

    tiles = [own] + [swap(own if dim else own_copy, sizes, dim, pairs) for dim, _, pairs in swaps]
    kept = jax.ShapeDtypeStruct((spans, rows, HEAD_SIZE), jnp.float32)
    result = jax.ShapeDtypeStruct((spans, tok_rows, width), bf16)
    state = ()
    cut = [0] + [n for n in CUTS if n < len(tiles)] + [len(tiles)]
    for start, stop in zip(cut, cut[1:], strict=False):
        numbers = tuple(range(start, stop))
        first, last = start == 0, stop == len(tiles)
        outs = [result] if last else [kept] * 3
        given = (q_all, *tiles[start:stop], *masks, *state)
        state = pl.pallas_call(
            functools.partial(attend, spans, sizes, ways, numbers),
            out_shape=outs,
            in_specs=[vmem()] * len(given),
            out_specs=[vmem()] * len(outs),
            scratch_shapes=[pltpu.VMEM((spans, rows, spans * len(numbers) * tok_rows), jnp.float32)],
            compiler_params=params,
            cost_estimate=pl.CostEstimate(
                flops=OWN_FLOPS if first else LATER_FLOPS, bytes_accessed=4_000_000, transcendentals=0
            ),
            name=f"attend_{start}",
        )(*given)
    outs = state[0]

    home = [outs[0]] + [None] * (spans - 1)
    places = [0, *range(1, spans - 2), *range(spans - 2, spans)[::-1]] if spans > 2 else list(range(spans))
    for k in order:
        home[k] = exchange(outs[k], k)
    attended = pl.pallas_call(
        functools.partial(join, places),
        out_shape=jax.ShapeDtypeStruct((tok_rows, spans * width), bf16),
        in_specs=[vmem()] * spans,
        out_specs=vmem(),
        compiler_params=params,
        name="join",
    )(*(home[k] for k in places))
    return attended.reshape(1, 1, 1, tok_rows, -1)


def solution(mesh):
    return jax.shard_map(
        shards,
        mesh=mesh,
        in_specs=(
            P("span", "ty", "tx", None, None),
            P("span", "ty", "tx", None, None),
            P("span", "ty", "tx", None),
            P(),
            P(),
        ),
        out_specs=P("span", "ty", "tx", None, None),
        check_vma=False,
    )
```

```python
import functools
import itertools
import math

import jax
import jax.numpy as jnp
from jax import lax
from jax.experimental import pallas as pl
from jax.experimental.pallas import tpu as pltpu
from jax.sharding import PartitionSpec as P

HEAD_SIZE = 128
NEIGH = 5
EXTRA = 16
OWN_FLOPS = 10_000_000_000
LATER_FLOPS = 1_000_000
CUTS = (1, 2)
SMALL = pl.CostEstimate(flops=1000, bytes_accessed=1000, transcendentals=0)
DEAD = -1e30
VMEM_LIMIT = 40 * 1024 * 1024


def vmem():
    return pl.BlockSpec(memory_space=pltpu.VMEM)


def smem():
    return pl.BlockSpec(memory_space=pltpu.SMEM)


def pairings(count):
    found = []
    for first in (0, 1):
        pairs = [(i, i + 1) for i in range(first, count - 1, 2)]
        if pairs:
            found.append(pairs)
    return found


def swap(block, sizes, dim, pairs):
    rows, cols = sizes
    paired = {i: j for a, b in pairs for i, j in ((a, b), (b, a))}
    moves = []
    for row in range(rows):
        for col in range(cols):
            place = [row, col]
            if place[dim] in paired:
                place[dim] = paired[place[dim]]
            elif dim == 1 and rows % 2 == 0:
                place[0] = row ^ 1
            else:
                continue
            moves.append((row * cols + col, place[0] * cols + place[1]))
    return lax.ppermute(block, ("ty", "tx"), moves)


def partner(place, count, first):
    low = lax.rem(place + first, 2) == 0
    step = jnp.where(low, 1, -1)
    other = place + step
    return jnp.where((other >= 0) & (other < count), step, 0)


def has_partner(place, sizes, way):
    other = place + 1 if (place + way[1]) % 2 == 0 else place - 1
    return 0 <= other < sizes[way[0]]


def split(spans, sizes, ways, *refs):
    (pattern_hbm, counts_hbm, mask_hbm, kv_hbm, q_hbm), refs = refs[:5], refs[5:]
    kv_refs, q_refs, refs = refs[:spans], refs[spans : 2 * spans], refs[2 * spans :]
    bias_ref, keep_ref, pattern_ref, counts_ref, mask_ref, kv_ref, q_ref, sems = refs
    me = lax.axis_index("span")
    at = [lax.axis_index(axis) for axis in ("ty", "tx")]
    kv_width = kv_hbm.shape[1] // 2
    rows = q_hbm.shape[0]
    width = q_hbm.shape[1] // spans
    copies = [
        pltpu.make_async_copy(source, target, sems.at[i])
        for i, (source, target) in enumerate(
            (
                (pattern_hbm, pattern_ref),
                (counts_hbm, counts_ref),
                (mask_hbm, mask_ref),
                (kv_hbm, kv_ref),
                (q_hbm, q_ref),
            )
        )
    ]
    for copy in copies:
        copy.start()
    for copy in copies[:3]:
        copy.wait()
    row_ids = lax.broadcasted_iota(jnp.int32, (EXTRA, width), 0)
    extra = jnp.zeros((EXTRA, width), jnp.float32)
    for o in range(NEIGH):
        extra = jnp.where(row_ids == o, pattern_ref[o].astype(jnp.float32), extra)
    extra = extra.astype(jnp.bfloat16)
    for k in range(spans):
        q_refs[k][rows:] = extra

    lanes = lax.broadcasted_iota(jnp.int32, (1, rows), 1)
    row_ids = lax.broadcasted_iota(jnp.int32, (rows, HEAD_SIZE), 0)

    def count(span, step_row, step_col):
        return counts_ref[span, at[0] + step_row, at[1] + step_col]

    for other in range(spans):
        keep_ref[other] = jnp.where(row_ids < count(other, 0, 0), 1.0, 0.0)
        for t, way in enumerate(ways):
            if way is None:
                near = count(other, 0, 0)
            else:
                step = partner(at[way[0]], sizes[way[0]], way[1])
                near = count(other, *((step, 0) if way[0] == 0 else (0, step)))
                near = jnp.where(step == 0, 0, near)
            for span in range(other, spans):
                seen = jnp.where(mask_ref[span, other] > 0, near, 0)
                bias_ref[span, t : t + 1, other * rows : (other + 1) * rows] = jnp.where(
                    lanes < seen, 0.0, DEAD
                )

    copies[3].wait()
    for k in range(spans):
        for part in range(2):
            start = pl.multiple_of(part * kv_width + (me ^ k) * HEAD_SIZE, HEAD_SIZE)
            kv_refs[k][part] = kv_ref[:, pl.ds(start, HEAD_SIZE)]
    copies[4].wait()
    for k in range(spans):
        q_refs[k][:rows] = q_ref[:, pl.ds(pl.multiple_of((me ^ k) * width, HEAD_SIZE), width)]


def attend(spans, sizes, ways, numbers, chosen, *refs):
    first, last = numbers[0] == 0, numbers[-1] == len(ways) - 1
    q_ref, refs = refs[0], refs[1:]
    tile_refs, refs = dict(zip(numbers, refs, strict=False)), refs[len(numbers) :]
    (bias_ref, keep_ref), refs = refs[:2], refs[2:]
    if not first:
        (top_in, sum_in, acc_in), refs = refs[:3], refs[3:]
    if last:
        (out_ref,), refs = refs[:1], refs[1:]
    else:
        (top_ref, sum_ref, acc_ref), refs = refs[:3], refs[3:]
    (score_ref,) = refs
    me = lax.axis_index("span")
    tok_rows = q_ref.shape[1] - EXTRA
    groups = q_ref.shape[2] // HEAD_SIZE
    factor = HEAD_SIZE ** (-0.5) * math.log2(math.e)

    def pattern_rows(n):
        if ways[n] is None:
            return 0, 0
        base = 1 + 2 * ways[n][0]
        return base, base + 1

    steps = {
        n: None
        if ways[n] is None
        else partner(lax.axis_index(("ty", "tx")[ways[n][0]]), sizes[ways[n][0]], ways[n][1])
        for n in numbers
    }

    def bias_of(span, used):
        extra = q_ref[me ^ span, tok_rows:, :HEAD_SIZE].astype(jnp.float32)
        parts = []
        for n in used:
            step = steps[n]
            low, high = pattern_rows(n)
            chosen = extra[low : low + 1]
            if step is not None:
                chosen = jnp.where(step > 0, extra[high : high + 1], chosen)
            closed = jnp.where(chosen > 0, 0.0, DEAD)
            for other in range(span + 1):
                lanes = slice(other * tok_rows, (other + 1) * tok_rows)
                parts.append(bias_ref[span, n : n + 1, lanes] + closed)
        return jnp.concatenate(parts, axis=1)

    def gathered(span, part, used):
        return jnp.concatenate([t[me ^ o, part] for t in map(tile_refs.get, used) for o in range(span + 1)], axis=0)

    def score(span, used):
        query = jnp.concatenate(
            [q_ref[me ^ span, :tok_rows, g * HEAD_SIZE : (g + 1) * HEAD_SIZE] for g in range(groups)],
            axis=0,
        )
        keys = gathered(span, 0, used)
        score_ref[span, :, : keys.shape[0]] = lax.dot_general(
            query, keys, (((1,), (1,)), ((), ())), preferred_element_type=jnp.float32
        )

    def weigh(span, used):
        values = gathered(span, 1, used)
        bias = bias_of(span, used)
        blocks = [slice(b, b + HEAD_SIZE) for b in range(0, values.shape[0], HEAD_SIZE)]
        for g in range(groups):
            rows = slice(g * tok_rows, (g + 1) * tok_rows)
            shape = (tok_rows, HEAD_SIZE)
            before = jnp.full(shape, DEAD, jnp.float32) if first else top_in[span, rows]
            top = before
            for lanes in blocks:
                top = jnp.maximum(top, score_ref[span, rows, lanes] + bias[:, lanes])
            top = jnp.broadcast_to(jnp.max(top, axis=1, keepdims=True), shape)
            total, weights = jnp.zeros(shape, jnp.float32), []
            for lanes in blocks:
                weight = jnp.exp2((score_ref[span, rows, lanes] + bias[:, lanes] - top) * factor)
                total = total + weight
                weights.append(weight.astype(jnp.bfloat16))
            result = jnp.dot(
                jnp.concatenate(weights, axis=1), values, preferred_element_type=jnp.float32
            )
            if not first:
                fade = jnp.exp2((before - top) * factor)
                total = total + sum_in[span, rows] * fade
                result = result + acc_in[span, rows] * fade
            if not last:
                top_ref[span, rows], sum_ref[span, rows], acc_ref[span, rows] = top, total, result
                continue
            share = 1.0 / jnp.sum(total, axis=1, keepdims=True)
            result = result * jnp.where(top > 0.5 * DEAD, share, jnp.nan)
            out_ref[me ^ span, :, g * HEAD_SIZE : (g + 1) * HEAD_SIZE] = jnp.where(
                keep_ref[span] > 0, result, 0.0
            ).astype(jnp.bfloat16)

    def run(some, used):
        score(some[0], used)
        for i, span in enumerate(some):
            if i + 1 < len(some):
                score(some[i + 1], used)
            weigh(span, used)

    members = {}
    for place in range(spans):
        members.setdefault(tuple(sorted(place ^ k for k in chosen)), []).append(place)
    borders = {
        tuple(n for n in numbers if ways[n] is None or has_partner(spot[ways[n][0]], sizes, ways[n]))
        for spot in itertools.product(*map(range, sizes))
    }
    for some, places in sorted(members.items()):
        for inside in sorted(borders):
            tests = [] if len(places) == spans else [[me == place for place in places]]
            if len(borders) > 1:
                tests += [[(steps[n] != 0) == (n in inside)] for n in numbers if steps[n] is not None]
            case = functools.partial(run, some, inside or numbers[:1])
            if tests:
                tests = [functools.reduce(jnp.logical_or, test) for test in tests]
                pl.when(functools.reduce(jnp.logical_and, tests))(case)
            else:
                case()


def collect(spans, own_ref, *refs):
    q_refs, (q_all_ref, copy_ref) = refs[:spans], refs[spans:]
    for k in range(spans):
        q_all_ref[k] = q_refs[k][...]
    copy_ref[...] = own_ref[...]


def join(places, *refs):
    me = lax.axis_index("span")
    out_ref = refs[-1]
    for k, ref in zip(places, refs, strict=False):
        width = ref.shape[1]
        start = pl.multiple_of((me ^ k) * width, HEAD_SIZE)
        out_ref[:, pl.ds(start, width)] = ref[...]


def shards(queries, key_value, pattern, counts, span_mask):
    spans, ty_count, tx_count = (lax.axis_size(a) for a in ("span", "ty", "tx"))
    tok_rows = queries.shape[3]
    kv_heads = key_value.shape[4] // (2 * HEAD_SIZE)
    assert kv_heads == spans and spans & (spans - 1) == 0
    width = queries.shape[4] // spans
    groups = width // HEAD_SIZE
    bf16 = jnp.bfloat16
    params = pltpu.CompilerParams(vmem_limit_bytes=VMEM_LIMIT)

    def exchange(block, k):
        return lax.ppermute(block, "span", [(i, i ^ k) for i in range(spans)])

    sizes = (ty_count, tx_count)
    order = sorted(range(1, spans), key=lambda k: -bin(k).count("1"))

    swaps = [
        (dim, first, pairs) for dim in (0, 1) for first, pairs in enumerate(pairings(sizes[dim]))
    ]
    ways = (None, *((dim, first) for dim, first, _ in swaps))
    piece = jax.ShapeDtypeStruct((2, tok_rows, HEAD_SIZE), bf16)
    pieces = pl.pallas_call(
        functools.partial(split, spans, sizes, ways),
        out_shape=[piece] * spans
        + [jax.ShapeDtypeStruct((tok_rows + EXTRA, width), bf16)] * spans
        + [
            jax.ShapeDtypeStruct((spans, 8, spans * tok_rows), jnp.float32),
            jax.ShapeDtypeStruct((spans, tok_rows, HEAD_SIZE), jnp.float32),
        ],
        in_specs=[pl.BlockSpec(memory_space=pltpu.HBM)] * 5,
        out_specs=[vmem()] * (2 * spans + 2),
        scratch_shapes=[
            pltpu.SMEM((NEIGH,), jnp.int32),
            pltpu.SMEM(counts.shape, jnp.int32),
            pltpu.SMEM(span_mask.shape, jnp.int32),
            pltpu.VMEM((tok_rows, 2 * kv_heads * HEAD_SIZE), bf16),
            pltpu.VMEM((tok_rows, spans * width), bf16),
            pltpu.SemaphoreType.DMA((5,)),
        ],
        compiler_params=params,
        name="split",
    )(
        *(
            pltpu.with_memory_space_constraint(x, pltpu.HBM)
            for x in (
                pattern.reshape(NEIGH),
                counts,
                span_mask,
                key_value.reshape(tok_rows, -1),
                queries.reshape(tok_rows, -1),
            )
        )
    )
    kv_pieces, q_pieces, masks = pieces[:spans], pieces[spans : 2 * spans], pieces[2 * spans :]

    column = [kv_pieces[0]] + [None] * (spans - 1)
    for k in order:
        column[k] = exchange(kv_pieces[k], k)
    own = jnp.stack(column)
    q_here = [q_pieces[0]] + [None] * (spans - 1)
    for k in order:
        q_here[k] = exchange(q_pieces[k], k)

    sizes = (ty_count, tx_count)
    rows = groups * tok_rows
    q_all, own_copy = pl.pallas_call(
        functools.partial(collect, spans),
        out_shape=[
            jax.ShapeDtypeStruct((spans, *q_here[0].shape), bf16),
            jax.ShapeDtypeStruct(own.shape, bf16),
        ],
        in_specs=[vmem()] * (1 + spans),
        out_specs=[vmem()] * 2,
        compiler_params=params,
        name="collect",
    )(own, *q_here)

    tiles = [own] + [swap(own if dim else own_copy, sizes, dim, pairs) for dim, _, pairs in swaps]
    kept = jax.ShapeDtypeStruct((spans, rows, HEAD_SIZE), jnp.float32)
    result = jax.ShapeDtypeStruct((spans, tok_rows, width), bf16)

    def stage(start, stop, chosen, state, flops, name):
        numbers = tuple(range(start, stop))
        last = stop == len(tiles)
        given = (q_all, *tiles[start:stop], *masks, *state)
        return pl.pallas_call(
            functools.partial(attend, spans, sizes, ways, numbers, chosen),
            out_shape=[result] if last else [kept] * 3,
            in_specs=[vmem()] * len(given),
            out_specs=[vmem()] * (1 if last else 3),
            scratch_shapes=[pltpu.VMEM((spans, rows, spans * len(numbers) * tok_rows), jnp.float32)],
            compiler_params=params,
            cost_estimate=pl.CostEstimate(flops=flops, bytes_accessed=4_000_000, transcendentals=0),
            name=name,
        )(*given)

    state = ()
    cut = [0] + [n for n in CUTS if n < len(tiles)] + [len(tiles)]
    for start, stop in zip(cut[:-2], cut[1:-1], strict=True):
        flops = OWN_FLOPS if start == 0 else LATER_FLOPS
        state = stage(start, stop, range(spans), state, flops, f"attend_{start}")
    outs = [None] * spans
    parts = [tuple(range(spans))]
    for i, part in enumerate(parts):
        done = stage(cut[-2], cut[-1], part, state, LATER_FLOPS, f"attend_last_{i}")[0]
        for k in part:
            outs[k] = done[k]

    home = [outs[0]] + [None] * (spans - 1)
    places = [0, *range(1, spans - 2), *range(spans - 2, spans)[::-1]] if spans > 2 else list(range(spans))
    for k in order:
        home[k] = exchange(outs[k], k)
    attended = pl.pallas_call(
        functools.partial(join, places),
        out_shape=jax.ShapeDtypeStruct((tok_rows, spans * width), bf16),
        in_specs=[vmem()] * spans,
        out_specs=vmem(),
        compiler_params=params,
        name="join",
    )(*(home[k] for k in places))
    return attended.reshape(1, 1, 1, tok_rows, -1)


def solution(mesh):
    return jax.shard_map(
        shards,
        mesh=mesh,
        in_specs=(
            P("span", "ty", "tx", None, None),
            P("span", "ty", "tx", None, None),
            P("span", "ty", "tx", None),
            P(),
            P(),
        ),
        out_specs=P("span", "ty", "tx", None, None),
        check_vma=False,
    )
```

```python
import functools
import itertools
import math

import jax
import jax.numpy as jnp
from jax import lax
from jax.experimental import pallas as pl
from jax.experimental.pallas import tpu as pltpu
from jax.sharding import PartitionSpec as P

HEAD_SIZE = 128
NEIGH = 5
EXTRA = 16
OWN_FLOPS = 10_000_000_000
LATER_FLOPS = 1_000_000
CUTS = (1, 2, 3)
SMALL = pl.CostEstimate(flops=1000, bytes_accessed=1000, transcendentals=0)
DEAD = -1e30
VMEM_LIMIT = 40 * 1024 * 1024


def vmem():
    return pl.BlockSpec(memory_space=pltpu.VMEM)


def smem():
    return pl.BlockSpec(memory_space=pltpu.SMEM)


def pairings(count):
    found = []
    for first in (0, 1):
        pairs = [(i, i + 1) for i in range(first, count - 1, 2)]
        if pairs:
            found.append(pairs)
    return found


def swap(block, sizes, dim, pairs):
    rows, cols = sizes
    paired = {i: j for a, b in pairs for i, j in ((a, b), (b, a))}
    moves = []
    for row in range(rows):
        for col in range(cols):
            place = [row, col]
            if place[dim] in paired:
                place[dim] = paired[place[dim]]
            elif dim == 1 and rows % 2 == 0:
                place[0] = row ^ 1
            else:
                continue
            moves.append((row * cols + col, place[0] * cols + place[1]))
    return lax.ppermute(block, ("ty", "tx"), moves)


def partner(place, count, first):
    low = lax.rem(place + first, 2) == 0
    step = jnp.where(low, 1, -1)
    other = place + step
    return jnp.where((other >= 0) & (other < count), step, 0)


def has_partner(place, sizes, way):
    other = place + 1 if (place + way[1]) % 2 == 0 else place - 1
    return 0 <= other < sizes[way[0]]


def split(spans, sizes, ways, *refs):
    (pattern_hbm, counts_hbm, mask_hbm, kv_hbm, q_hbm), refs = refs[:5], refs[5:]
    kv_refs, q_refs, refs = refs[:spans], refs[spans : 2 * spans], refs[2 * spans :]
    bias_ref, keep_ref, pattern_ref, counts_ref, mask_ref, kv_ref, q_ref, sems = refs
    me = lax.axis_index("span")
    at = [lax.axis_index(axis) for axis in ("ty", "tx")]
    kv_width = kv_hbm.shape[1] // 2
    rows = q_hbm.shape[0]
    width = q_hbm.shape[1] // spans
    copies = [
        pltpu.make_async_copy(source, target, sems.at[i])
        for i, (source, target) in enumerate(
            (
                (pattern_hbm, pattern_ref),
                (counts_hbm, counts_ref),
                (mask_hbm, mask_ref),
                (kv_hbm, kv_ref),
                (q_hbm, q_ref),
            )
        )
    ]
    for copy in copies:
        copy.start()
    for copy in copies[:3]:
        copy.wait()
    row_ids = lax.broadcasted_iota(jnp.int32, (EXTRA, width), 0)
    extra = jnp.zeros((EXTRA, width), jnp.float32)
    for o in range(NEIGH):
        extra = jnp.where(row_ids == o, pattern_ref[o].astype(jnp.float32), extra)
    extra = extra.astype(jnp.bfloat16)
    for k in range(spans):
        q_refs[k][rows:] = extra

    lanes = lax.broadcasted_iota(jnp.int32, (1, rows), 1)
    row_ids = lax.broadcasted_iota(jnp.int32, (rows, HEAD_SIZE), 0)

    def count(span, step_row, step_col):
        return counts_ref[span, at[0] + step_row, at[1] + step_col]

    for other in range(spans):
        keep_ref[other] = jnp.where(row_ids < count(other, 0, 0), 1.0, 0.0)
        for t, way in enumerate(ways):
            if way is None:
                near = count(other, 0, 0)
            else:
                step = partner(at[way[0]], sizes[way[0]], way[1])
                near = count(other, *((step, 0) if way[0] == 0 else (0, step)))
                near = jnp.where(step == 0, 0, near)
            for span in range(other, spans):
                seen = jnp.where(mask_ref[span, other] > 0, near, 0)
                bias_ref[span, t : t + 1, other * rows : (other + 1) * rows] = jnp.where(
                    lanes < seen, 0.0, DEAD
                )

    copies[3].wait()
    for k in range(spans):
        for part in range(2):
            start = pl.multiple_of(part * kv_width + (me ^ k) * HEAD_SIZE, HEAD_SIZE)
            kv_refs[k][part] = kv_ref[:, pl.ds(start, HEAD_SIZE)]
    copies[4].wait()
    for k in range(spans):
        q_refs[k][:rows] = q_ref[:, pl.ds(pl.multiple_of((me ^ k) * width, HEAD_SIZE), width)]


def attend(spans, sizes, ways, numbers, chosen, *refs):
    first, last = numbers[0] == 0, numbers[-1] == len(ways) - 1
    q_ref, refs = refs[0], refs[1:]
    tile_refs, refs = dict(zip(numbers, refs, strict=False)), refs[len(numbers) :]
    (bias_ref, keep_ref), refs = refs[:2], refs[2:]
    if not first:
        (top_in, sum_in, acc_in), refs = refs[:3], refs[3:]
    if last:
        (out_ref,), refs = refs[:1], refs[1:]
    else:
        (top_ref, sum_ref, acc_ref), refs = refs[:3], refs[3:]
    (score_ref,) = refs
    me = lax.axis_index("span")
    tok_rows = q_ref.shape[1] - EXTRA
    groups = q_ref.shape[2] // HEAD_SIZE
    factor = HEAD_SIZE ** (-0.5) * math.log2(math.e)

    def pattern_rows(n):
        if ways[n] is None:
            return 0, 0
        base = 1 + 2 * ways[n][0]
        return base, base + 1

    steps = {
        n: None
        if ways[n] is None
        else partner(lax.axis_index(("ty", "tx")[ways[n][0]]), sizes[ways[n][0]], ways[n][1])
        for n in numbers
    }

    def bias_of(span, used):
        extra = q_ref[me ^ span, tok_rows:, :HEAD_SIZE].astype(jnp.float32)
        parts = []
        for n in used:
            step = steps[n]
            low, high = pattern_rows(n)
            chosen = extra[low : low + 1]
            if step is not None:
                chosen = jnp.where(step > 0, extra[high : high + 1], chosen)
            closed = jnp.where(chosen > 0, 0.0, DEAD)
            for other in range(span + 1):
                lanes = slice(other * tok_rows, (other + 1) * tok_rows)
                parts.append(bias_ref[span, n : n + 1, lanes] + closed)
        return jnp.concatenate(parts, axis=1)

    def gathered(span, part, used):
        return jnp.concatenate([t[me ^ o, part] for t in map(tile_refs.get, used) for o in range(span + 1)], axis=0)

    def score(span, used):
        query = jnp.concatenate(
            [q_ref[me ^ span, :tok_rows, g * HEAD_SIZE : (g + 1) * HEAD_SIZE] for g in range(groups)],
            axis=0,
        )
        keys = gathered(span, 0, used)
        score_ref[span, :, : keys.shape[0]] = lax.dot_general(
            query, keys, (((1,), (1,)), ((), ())), preferred_element_type=jnp.float32
        )

    def weigh(span, used):
        if used:
            values = gathered(span, 1, used)
            bias = bias_of(span, used)
            blocks = [slice(b, b + HEAD_SIZE) for b in range(0, values.shape[0], HEAD_SIZE)]
        for g in range(groups):
            rows = slice(g * tok_rows, (g + 1) * tok_rows)
            shape = (tok_rows, HEAD_SIZE)
            if used:
                before = jnp.full(shape, DEAD, jnp.float32) if first else top_in[span, rows]
                top = before
                for lanes in blocks:
                    top = jnp.maximum(top, score_ref[span, rows, lanes] + bias[:, lanes])
                top = jnp.broadcast_to(jnp.max(top, axis=1, keepdims=True), shape)
                total, weights = jnp.zeros(shape, jnp.float32), []
                for lanes in blocks:
                    weight = jnp.exp2((score_ref[span, rows, lanes] + bias[:, lanes] - top) * factor)
                    total = total + weight
                    weights.append(weight.astype(jnp.bfloat16))
                result = jnp.dot(
                    jnp.concatenate(weights, axis=1), values, preferred_element_type=jnp.float32
                )
                if not first:
                    fade = jnp.exp2((before - top) * factor)
                    total = total + sum_in[span, rows] * fade
                    result = result + acc_in[span, rows] * fade
            else:
                top, total, result = top_in[span, rows], sum_in[span, rows], acc_in[span, rows]
            if not last:
                top_ref[span, rows], sum_ref[span, rows], acc_ref[span, rows] = top, total, result
                continue
            share = 1.0 / jnp.sum(total, axis=1, keepdims=True)
            result = result * jnp.where(top > 0.5 * DEAD, share, jnp.nan)
            out_ref[me ^ span, :, g * HEAD_SIZE : (g + 1) * HEAD_SIZE] = jnp.where(
                keep_ref[span] > 0, result, 0.0
            ).astype(jnp.bfloat16)

    def run(some, used):
        if used:
            score(some[0], used)
        for i, span in enumerate(some):
            if used and i + 1 < len(some):
                score(some[i + 1], used)
            weigh(span, used)

    members = {}
    for place in range(spans):
        members.setdefault(tuple(sorted(place ^ k for k in chosen)), []).append(place)
    borders = {
        tuple(n for n in numbers if ways[n] is None or has_partner(spot[ways[n][0]], sizes, ways[n]))
        for spot in itertools.product(*map(range, sizes))
    }
    for some, places in sorted(members.items()):
        for inside in sorted(borders):
            tests = [] if len(places) == spans else [[me == place for place in places]]
            if len(borders) > 1:
                tests += [[(steps[n] != 0) == (n in inside)] for n in numbers if steps[n] is not None]
            case = functools.partial(run, some, inside)
            if tests:
                tests = [functools.reduce(jnp.logical_or, test) for test in tests]
                pl.when(functools.reduce(jnp.logical_and, tests))(case)
            else:
                case()


def collect(spans, *refs):
    for k in range(spans):
        refs[spans][k] = refs[k][...]


def copy(own_ref, after_ref, copy_ref):
    copy_ref[...] = own_ref[...]


def join(places, *refs):
    me = lax.axis_index("span")
    out_ref = refs[-1]
    for k, ref in zip(places, refs, strict=False):
        width = ref.shape[1]
        start = pl.multiple_of((me ^ k) * width, HEAD_SIZE)
        out_ref[:, pl.ds(start, width)] = ref[...]


def shards(queries, key_value, pattern, counts, span_mask):
    spans, ty_count, tx_count = (lax.axis_size(a) for a in ("span", "ty", "tx"))
    tok_rows = queries.shape[3]
    kv_heads = key_value.shape[4] // (2 * HEAD_SIZE)
    assert kv_heads == spans and spans & (spans - 1) == 0
    width = queries.shape[4] // spans
    groups = width // HEAD_SIZE
    bf16 = jnp.bfloat16
    params = pltpu.CompilerParams(vmem_limit_bytes=VMEM_LIMIT)

    def exchange(block, k):
        return lax.ppermute(block, "span", [(i, i ^ k) for i in range(spans)])

    sizes = (ty_count, tx_count)
    order = sorted(range(1, spans), key=lambda k: -bin(k).count("1"))

    swaps = [
        (dim, first, pairs) for dim in (0, 1) for first, pairs in enumerate(pairings(sizes[dim]))
    ]
    ways = (None, *((dim, first) for dim, first, _ in swaps))
    piece = jax.ShapeDtypeStruct((2, tok_rows, HEAD_SIZE), bf16)
    pieces = pl.pallas_call(
        functools.partial(split, spans, sizes, ways),
        out_shape=[piece] * spans
        + [jax.ShapeDtypeStruct((tok_rows + EXTRA, width), bf16)] * spans
        + [
            jax.ShapeDtypeStruct((spans, 8, spans * tok_rows), jnp.float32),
            jax.ShapeDtypeStruct((spans, tok_rows, HEAD_SIZE), jnp.float32),
        ],
        in_specs=[pl.BlockSpec(memory_space=pltpu.HBM)] * 5,
        out_specs=[vmem()] * (2 * spans + 2),
        scratch_shapes=[
            pltpu.SMEM((NEIGH,), jnp.int32),
            pltpu.SMEM(counts.shape, jnp.int32),
            pltpu.SMEM(span_mask.shape, jnp.int32),
            pltpu.VMEM((tok_rows, 2 * kv_heads * HEAD_SIZE), bf16),
            pltpu.VMEM((tok_rows, spans * width), bf16),
            pltpu.SemaphoreType.DMA((5,)),
        ],
        compiler_params=params,
        name="split",
    )(
        *(
            pltpu.with_memory_space_constraint(x, pltpu.HBM)
            for x in (
                pattern.reshape(NEIGH),
                counts,
                span_mask,
                key_value.reshape(tok_rows, -1),
                queries.reshape(tok_rows, -1),
            )
        )
    )
    kv_pieces, q_pieces, masks = pieces[:spans], pieces[spans : 2 * spans], pieces[2 * spans :]

    column = [kv_pieces[0]] + [None] * (spans - 1)
    for k in order:
        column[k] = exchange(kv_pieces[k], k)
    own = jnp.stack(column)
    q_here = [q_pieces[0]] + [None] * (spans - 1)
    for k in order:
        q_here[k] = exchange(q_pieces[k], k)

    sizes = (ty_count, tx_count)
    rows = groups * tok_rows
    own_copy = pl.pallas_call(
        copy,
        out_shape=jax.ShapeDtypeStruct(own.shape, bf16),
        in_specs=[vmem()] * 2,
        out_specs=vmem(),
        compiler_params=params,
        cost_estimate=SMALL,
        name="copy",
    )(own, q_here[1])
    q_all = pl.pallas_call(
        functools.partial(collect, spans),
        out_shape=jax.ShapeDtypeStruct((spans, *q_here[0].shape), bf16),
        in_specs=[vmem()] * spans,
        out_specs=vmem(),
        compiler_params=params,
        cost_estimate=SMALL,
        name="collect",
    )(*q_here)
    tiles = [own] + [swap(own if dim else own_copy, sizes, dim, pairs) for dim, _, pairs in swaps]
    kept = jax.ShapeDtypeStruct((spans, rows, HEAD_SIZE), jnp.float32)
    result = jax.ShapeDtypeStruct((spans, tok_rows, width), bf16)

    def stage(start, stop, chosen, state, flops, name):
        numbers = tuple(range(start, stop))
        last = stop == len(tiles)
        given = (q_all, *tiles[start:stop], *masks, *state)
        return pl.pallas_call(
            functools.partial(attend, spans, sizes, ways, numbers, chosen),
            out_shape=[result] if last else [kept] * 3,
            in_specs=[vmem()] * len(given),
            out_specs=[vmem()] * (1 if last else 3),
            scratch_shapes=[pltpu.VMEM((spans, rows, spans * len(numbers) * tok_rows), jnp.float32)],
            compiler_params=params,
            cost_estimate=pl.CostEstimate(flops=flops, bytes_accessed=4_000_000, transcendentals=0),
            name=name,
        )(*given)

    state = ()
    cut = [0] + [n for n in CUTS if n < len(tiles)] + [len(tiles)]
    for start, stop in zip(cut[:-2], cut[1:-1], strict=True):
        flops = OWN_FLOPS if start == 0 else LATER_FLOPS
        state = stage(start, stop, range(spans), state, flops, f"attend_{start}")
    outs = [None] * spans
    parts = [tuple(range(spans))]
    for i, part in enumerate(parts):
        done = stage(cut[-2], cut[-1], part, state, LATER_FLOPS, f"attend_last_{i}")[0]
        for k in part:
            outs[k] = done[k]

    home = [outs[0]] + [None] * (spans - 1)
    places = [0, *range(1, spans - 2), *range(spans - 2, spans)[::-1]] if spans > 2 else list(range(spans))
    for k in order:
        home[k] = exchange(outs[k], k)
    attended = pl.pallas_call(
        functools.partial(join, places),
        out_shape=jax.ShapeDtypeStruct((tok_rows, spans * width), bf16),
        in_specs=[vmem()] * spans,
        out_specs=vmem(),
        compiler_params=params,
        name="join",
    )(*(home[k] for k in places))
    return attended.reshape(1, 1, 1, tok_rows, -1)


def solution(mesh):
    return jax.shard_map(
        shards,
        mesh=mesh,
        in_specs=(
            P("span", "ty", "tx", None, None),
            P("span", "ty", "tx", None, None),
            P("span", "ty", "tx", None),
            P(),
            P(),
        ),
        out_specs=P("span", "ty", "tx", None, None),
        check_vma=False,
    )
```

```python
import functools
import itertools
import math

import jax
import jax.numpy as jnp
from jax import lax
from jax.experimental import pallas as pl
from jax.experimental.pallas import tpu as pltpu
from jax.sharding import PartitionSpec as P

HEAD_SIZE = 128
NEIGH = 5
EXTRA = 16
OWN_FLOPS = 10_000_000_000
LATER_FLOPS = 1_000_000
CUTS = (1, 2, 3)
SMALL = pl.CostEstimate(flops=1000, bytes_accessed=1000, transcendentals=0)
DEAD = -1e30
VMEM_LIMIT = 40 * 1024 * 1024


def vmem():
    return pl.BlockSpec(memory_space=pltpu.VMEM)


def smem():
    return pl.BlockSpec(memory_space=pltpu.SMEM)


def pairings(count):
    found = []
    for first in (0, 1):
        pairs = [(i, i + 1) for i in range(first, count - 1, 2)]
        if pairs:
            found.append(pairs)
    return found


def swap(block, sizes, dim, pairs):
    rows, cols = sizes
    paired = {i: j for a, b in pairs for i, j in ((a, b), (b, a))}
    moves = []
    for row in range(rows):
        for col in range(cols):
            place = [row, col]
            if place[dim] in paired:
                place[dim] = paired[place[dim]]
            elif dim == 1 and rows % 2 == 0:
                place[0] = row ^ 1
            else:
                continue
            moves.append((row * cols + col, place[0] * cols + place[1]))
    return lax.ppermute(block, ("ty", "tx"), moves)


def partner(place, count, first):
    low = lax.rem(place + first, 2) == 0
    step = jnp.where(low, 1, -1)
    other = place + step
    return jnp.where((other >= 0) & (other < count), step, 0)


def has_partner(place, sizes, way):
    other = place + 1 if (place + way[1]) % 2 == 0 else place - 1
    return 0 <= other < sizes[way[0]]


def split(spans, sizes, ways, *refs):
    (pattern_hbm, counts_hbm, mask_hbm, kv_hbm, q_hbm), refs = refs[:5], refs[5:]
    kv_refs, q_refs, refs = refs[:spans], refs[spans : 2 * spans], refs[2 * spans :]
    bias_ref, keep_ref, pattern_ref, counts_ref, mask_ref, kv_ref, q_ref, sems = refs
    me = lax.axis_index("span")
    at = [lax.axis_index(axis) for axis in ("ty", "tx")]
    kv_width = kv_hbm.shape[1] // 2
    rows = q_hbm.shape[0]
    width = q_hbm.shape[1] // spans
    copies = [
        pltpu.make_async_copy(source, target, sems.at[i])
        for i, (source, target) in enumerate(
            (
                (pattern_hbm, pattern_ref),
                (counts_hbm, counts_ref),
                (mask_hbm, mask_ref),
                (kv_hbm, kv_ref),
                (q_hbm, q_ref),
            )
        )
    ]
    for copy in copies:
        copy.start()
    for copy in copies[:3]:
        copy.wait()
    row_ids = lax.broadcasted_iota(jnp.int32, (EXTRA, width), 0)
    extra = jnp.zeros((EXTRA, width), jnp.float32)
    for o in range(NEIGH):
        extra = jnp.where(row_ids == o, pattern_ref[o].astype(jnp.float32), extra)
    extra = extra.astype(jnp.bfloat16)
    for k in range(spans):
        q_refs[k][rows:] = extra

    lanes = lax.broadcasted_iota(jnp.int32, (1, rows), 1)
    row_ids = lax.broadcasted_iota(jnp.int32, (rows, HEAD_SIZE), 0)

    def count(span, step_row, step_col):
        return counts_ref[span, at[0] + step_row, at[1] + step_col]

    for other in range(spans):
        keep_ref[other] = jnp.where(row_ids < count(other, 0, 0), 1.0, 0.0)
        for t, way in enumerate(ways):
            if way is None:
                near = count(other, 0, 0)
            else:
                step = partner(at[way[0]], sizes[way[0]], way[1])
                near = count(other, *((step, 0) if way[0] == 0 else (0, step)))
                near = jnp.where(step == 0, 0, near)
            for span in range(other, spans):
                seen = jnp.where(mask_ref[span, other] > 0, near, 0)
                bias_ref[span, t : t + 1, other * rows : (other + 1) * rows] = jnp.where(
                    lanes < seen, 0.0, DEAD
                )

    copies[3].wait()
    for k in range(spans):
        for part in range(2):
            start = pl.multiple_of(part * kv_width + (me ^ k) * HEAD_SIZE, HEAD_SIZE)
            kv_refs[k][part] = kv_ref[:, pl.ds(start, HEAD_SIZE)]
    copies[4].wait()
    for k in range(spans):
        q_refs[k][:rows] = q_ref[:, pl.ds(pl.multiple_of((me ^ k) * width, HEAD_SIZE), width)]


def attend(spans, sizes, ways, numbers, chosen, *refs):
    first, last = numbers[0] == 0, numbers[-1] == len(ways) - 1
    q_ref, refs = refs[0], refs[1:]
    tile_refs, refs = dict(zip(numbers, refs, strict=False)), refs[len(numbers) :]
    (bias_ref, keep_ref), refs = refs[:2], refs[2:]
    if not first:
        (top_in, sum_in, acc_in), refs = refs[:3], refs[3:]
    if last:
        (out_ref,), refs = refs[:1], refs[1:]
    else:
        (top_ref, sum_ref, acc_ref), refs = refs[:3], refs[3:]
    (score_ref,) = refs
    me = lax.axis_index("span")
    tok_rows = q_ref.shape[1] - EXTRA
    groups = q_ref.shape[2] // HEAD_SIZE
    factor = HEAD_SIZE ** (-0.5) * math.log2(math.e)

    def pattern_rows(n):
        if ways[n] is None:
            return 0, 0
        base = 1 + 2 * ways[n][0]
        return base, base + 1

    steps = {
        n: None
        if ways[n] is None
        else partner(lax.axis_index(("ty", "tx")[ways[n][0]]), sizes[ways[n][0]], ways[n][1])
        for n in numbers
    }

    def bias_of(span, used):
        extra = q_ref[me ^ span, tok_rows:, :HEAD_SIZE].astype(jnp.float32)
        parts = []
        for n in used:
            step = steps[n]
            low, high = pattern_rows(n)
            chosen = extra[low : low + 1]
            if step is not None:
                chosen = jnp.where(step > 0, extra[high : high + 1], chosen)
            closed = jnp.where(chosen > 0, 0.0, DEAD)
            for other in range(span + 1):
                lanes = slice(other * tok_rows, (other + 1) * tok_rows)
                parts.append(bias_ref[span, n : n + 1, lanes] + closed)
        return jnp.concatenate(parts, axis=1)

    def gathered(span, part, used):
        return jnp.concatenate([t[me ^ o, part] for t in map(tile_refs.get, used) for o in range(span + 1)], axis=0)

    def score(span, used):
        query = jnp.concatenate(
            [q_ref[me ^ span, :tok_rows, g * HEAD_SIZE : (g + 1) * HEAD_SIZE] for g in range(groups)],
            axis=0,
        )
        keys = gathered(span, 0, used)
        score_ref[span, :, : keys.shape[0]] = lax.dot_general(
            query, keys, (((1,), (1,)), ((), ())), preferred_element_type=jnp.float32
        )

    def weigh(span, used):
        if used:
            values = gathered(span, 1, used)
            bias = bias_of(span, used)
            blocks = [slice(b, b + HEAD_SIZE) for b in range(0, values.shape[0], HEAD_SIZE)]
        for g in range(groups):
            rows = slice(g * tok_rows, (g + 1) * tok_rows)
            shape = (tok_rows, HEAD_SIZE)
            if used:
                before = jnp.full(shape, DEAD, jnp.float32) if first else top_in[span, rows]
                top = before
                for lanes in blocks:
                    top = jnp.maximum(top, score_ref[span, rows, lanes] + bias[:, lanes])
                top = jnp.broadcast_to(jnp.max(top, axis=1, keepdims=True), shape)
                total, weights = jnp.zeros(shape, jnp.float32), []
                for lanes in blocks:
                    weight = jnp.exp2((score_ref[span, rows, lanes] + bias[:, lanes] - top) * factor)
                    total = total + weight
                    weights.append(weight.astype(jnp.bfloat16))
                result = jnp.dot(
                    jnp.concatenate(weights, axis=1), values, preferred_element_type=jnp.float32
                )
                if not first:
                    fade = jnp.exp2((before - top) * factor)
                    total = total + sum_in[span, rows] * fade
                    result = result + acc_in[span, rows] * fade
            else:
                top, total, result = top_in[span, rows], sum_in[span, rows], acc_in[span, rows]
            if not last:
                top_ref[span, rows], sum_ref[span, rows], acc_ref[span, rows] = top, total, result
                continue
            share = 1.0 / jnp.sum(total, axis=1, keepdims=True)
            result = result * jnp.where(top > 0.5 * DEAD, share, jnp.nan)
            out_ref[me ^ span, :, g * HEAD_SIZE : (g + 1) * HEAD_SIZE] = jnp.where(
                keep_ref[span] > 0, result, 0.0
            ).astype(jnp.bfloat16)

    def run(some, used):
        if used:
            score(some[0], used)
        for i, span in enumerate(some):
            if used and i + 1 < len(some):
                score(some[i + 1], used)
            weigh(span, used)

    members = {}
    for place in range(spans):
        members.setdefault(tuple(sorted(place ^ k for k in chosen)), []).append(place)
    borders = {
        tuple(n for n in numbers if ways[n] is None or has_partner(spot[ways[n][0]], sizes, ways[n]))
        for spot in itertools.product(*map(range, sizes))
    }
    for some, places in sorted(members.items()):
        for inside in sorted(borders):
            tests = [] if len(places) == spans else [[me == place for place in places]]
            if len(borders) > 1:
                tests += [[(steps[n] != 0) == (n in inside)] for n in numbers if steps[n] is not None]
            case = functools.partial(run, some, inside)
            if tests:
                tests = [functools.reduce(jnp.logical_or, test) for test in tests]
                pl.when(functools.reduce(jnp.logical_and, tests))(case)
            else:
                case()


def collect(spans, *refs):
    for k in range(spans):
        refs[spans][k] = refs[k][...]


def copy(own_ref, after_ref, copy_ref):
    copy_ref[...] = own_ref[...]


def join(places, *refs):
    me = lax.axis_index("span")
    out_ref = refs[-1]
    for k, ref in zip(places, refs, strict=False):
        width = ref.shape[1]
        start = pl.multiple_of((me ^ k) * width, HEAD_SIZE)
        out_ref[:, pl.ds(start, width)] = ref[...]


def shards(queries, key_value, pattern, counts, span_mask):
    spans, ty_count, tx_count = (lax.axis_size(a) for a in ("span", "ty", "tx"))
    tok_rows = queries.shape[3]
    kv_heads = key_value.shape[4] // (2 * HEAD_SIZE)
    assert kv_heads == spans and spans & (spans - 1) == 0
    width = queries.shape[4] // spans
    groups = width // HEAD_SIZE
    bf16 = jnp.bfloat16
    params = pltpu.CompilerParams(vmem_limit_bytes=VMEM_LIMIT)

    def exchange(block, k):
        return lax.ppermute(block, "span", [(i, i ^ k) for i in range(spans)])

    sizes = (ty_count, tx_count)
    order = sorted(range(1, spans), key=lambda k: -bin(k).count("1"))

    swaps = [
        (dim, first, pairs) for dim in (0, 1) for first, pairs in enumerate(pairings(sizes[dim]))
    ]
    ways = (None, *((dim, first) for dim, first, _ in swaps))
    piece = jax.ShapeDtypeStruct((2, tok_rows, HEAD_SIZE), bf16)
    pieces = pl.pallas_call(
        functools.partial(split, spans, sizes, ways),
        out_shape=[piece] * spans
        + [jax.ShapeDtypeStruct((tok_rows + EXTRA, width), bf16)] * spans
        + [
            jax.ShapeDtypeStruct((spans, 8, spans * tok_rows), jnp.float32),
            jax.ShapeDtypeStruct((spans, tok_rows, HEAD_SIZE), jnp.float32),
        ],
        in_specs=[pl.BlockSpec(memory_space=pltpu.HBM)] * 5,
        out_specs=[vmem()] * (2 * spans + 2),
        scratch_shapes=[
            pltpu.SMEM((NEIGH,), jnp.int32),
            pltpu.SMEM(counts.shape, jnp.int32),
            pltpu.SMEM(span_mask.shape, jnp.int32),
            pltpu.VMEM((tok_rows, 2 * kv_heads * HEAD_SIZE), bf16),
            pltpu.VMEM((tok_rows, spans * width), bf16),
            pltpu.SemaphoreType.DMA((5,)),
        ],
        compiler_params=params,
        name="split",
    )(
        *(
            pltpu.with_memory_space_constraint(x, pltpu.HBM)
            for x in (
                pattern.reshape(NEIGH),
                counts,
                span_mask,
                key_value.reshape(tok_rows, -1),
                queries.reshape(tok_rows, -1),
            )
        )
    )
    kv_pieces, q_pieces, masks = pieces[:spans], pieces[spans : 2 * spans], pieces[2 * spans :]

    column = [kv_pieces[0]] + [None] * (spans - 1)
    for k in order:
        column[k] = exchange(kv_pieces[k], k)
    own = jnp.stack(column)
    q_here = [q_pieces[0]] + [None] * (spans - 1)
    for k in order:
        q_here[k] = exchange(q_pieces[k], k)

    sizes = (ty_count, tx_count)
    rows = groups * tok_rows
    own_copy = pl.pallas_call(
        copy,
        out_shape=jax.ShapeDtypeStruct(own.shape, bf16),
        in_specs=[vmem()] * 2,
        out_specs=vmem(),
        compiler_params=params,
        cost_estimate=SMALL,
        name="copy",
    )(own, q_here[1])
    q_all = pl.pallas_call(
        functools.partial(collect, spans),
        out_shape=jax.ShapeDtypeStruct((spans, *q_here[0].shape), bf16),
        in_specs=[vmem()] * spans,
        out_specs=vmem(),
        compiler_params=params,
        cost_estimate=SMALL,
        name="collect",
    )(*q_here)
    tiles = [own] + [swap(own if dim else own_copy, sizes, dim, pairs) for dim, _, pairs in swaps]
    kept = jax.ShapeDtypeStruct((spans, rows, HEAD_SIZE), jnp.float32)
    result = jax.ShapeDtypeStruct((spans, tok_rows, width), bf16)

    def stage(start, stop, chosen, state, flops, name):
        numbers = tuple(range(start, stop))
        last = stop == len(tiles)
        given = (q_all, *tiles[start:stop], *masks, *state)
        return pl.pallas_call(
            functools.partial(attend, spans, sizes, ways, numbers, chosen),
            out_shape=[result] if last else [kept] * 3,
            in_specs=[vmem()] * len(given),
            out_specs=[vmem()] * (1 if last else 3),
            scratch_shapes=[pltpu.VMEM((spans, rows, spans * len(numbers) * tok_rows), jnp.float32)],
            compiler_params=params,
            cost_estimate=pl.CostEstimate(flops=flops, bytes_accessed=4_000_000, transcendentals=0),
            name=name,
        )(*given)

    state = ()
    cut = [0] + [n for n in CUTS if n < len(tiles)] + [len(tiles)]
    for start, stop in zip(cut[:-2], cut[1:-1], strict=True):
        flops = OWN_FLOPS if start == 0 else LATER_FLOPS
        state = stage(start, stop, range(spans), state, flops, f"attend_{start}")
    outs = [None] * spans
    parts = [tuple(range(spans))]
    for i, part in enumerate(parts):
        done = stage(cut[-2], cut[-1], part, state, LATER_FLOPS, f"attend_last_{i}")[0]
        for k in part:
            outs[k] = done[k]

    home = [outs[0]] + [None] * (spans - 1)
    places = [0, *range(2, spans), 1] if spans > 2 else list(range(spans))
    for k in order:
        home[k] = exchange(outs[k], k)
    attended = pl.pallas_call(
        functools.partial(join, places),
        out_shape=jax.ShapeDtypeStruct((tok_rows, spans * width), bf16),
        in_specs=[vmem()] * spans,
        out_specs=vmem(),
        compiler_params=params,
        name="join",
    )(*(home[k] for k in places))
    return attended.reshape(1, 1, 1, tok_rows, -1)


def solution(mesh):
    return jax.shard_map(
        shards,
        mesh=mesh,
        in_specs=(
            P("span", "ty", "tx", None, None),
            P("span", "ty", "tx", None, None),
            P("span", "ty", "tx", None),
            P(),
            P(),
        ),
        out_specs=P("span", "ty", "tx", None, None),
        check_vma=False,
    )
```

```python
import functools
import itertools
import math

import jax
import jax.numpy as jnp
from jax import lax
from jax.experimental import pallas as pl
from jax.experimental.pallas import tpu as pltpu
from jax.sharding import PartitionSpec as P

HEAD_SIZE = 128
NEIGH = 5
EXTRA = 16
OWN_FLOPS = 10_000_000_000
LATER_FLOPS = 1_000_000
CUTS = (1, 2, 3)
SMALL = pl.CostEstimate(flops=1000, bytes_accessed=1000, transcendentals=0)
DEAD = -1e30
VMEM_LIMIT = 40 * 1024 * 1024


def vmem():
    return pl.BlockSpec(memory_space=pltpu.VMEM)


def smem():
    return pl.BlockSpec(memory_space=pltpu.SMEM)


def pairings(count):
    found = []
    for first in (0, 1):
        pairs = [(i, i + 1) for i in range(first, count - 1, 2)]
        if pairs:
            found.append(pairs)
    return found


def swap(block, sizes, dim, pairs):
    rows, cols = sizes
    paired = {i: j for a, b in pairs for i, j in ((a, b), (b, a))}
    moves = []
    for row in range(rows):
        for col in range(cols):
            place = [row, col]
            if place[dim] in paired:
                place[dim] = paired[place[dim]]
            elif dim == 1 and rows % 2 == 0:
                place[0] = row ^ 1
            else:
                continue
            moves.append((row * cols + col, place[0] * cols + place[1]))
    return lax.ppermute(block, ("ty", "tx"), moves)


def partner(place, count, first):
    low = lax.rem(place + first, 2) == 0
    step = jnp.where(low, 1, -1)
    other = place + step
    return jnp.where((other >= 0) & (other < count), step, 0)


def has_partner(place, sizes, way):
    other = place + 1 if (place + way[1]) % 2 == 0 else place - 1
    return 0 <= other < sizes[way[0]]


def split(spans, sizes, ways, *refs):
    (pattern_hbm, counts_hbm, mask_hbm, kv_hbm, q_hbm), refs = refs[:5], refs[5:]
    kv_refs, q_refs, refs = refs[:spans], refs[spans : 2 * spans], refs[2 * spans :]
    bias_ref, keep_ref, pattern_ref, counts_ref, mask_ref, kv_ref, q_ref, sems = refs
    me = lax.axis_index("span")
    at = [lax.axis_index(axis) for axis in ("ty", "tx")]
    kv_width = kv_hbm.shape[1] // 2
    rows = q_hbm.shape[0]
    width = q_hbm.shape[1] // spans
    copies = [
        pltpu.make_async_copy(source, target, sems.at[i])
        for i, (source, target) in enumerate(
            (
                (pattern_hbm, pattern_ref),
                (counts_hbm, counts_ref),
                (mask_hbm, mask_ref),
                (kv_hbm, kv_ref),
                (q_hbm, q_ref),
            )
        )
    ]
    for copy in copies:
        copy.start()
    for copy in copies[:3]:
        copy.wait()
    row_ids = lax.broadcasted_iota(jnp.int32, (EXTRA, width), 0)
    extra = jnp.zeros((EXTRA, width), jnp.float32)
    for o in range(NEIGH):
        extra = jnp.where(row_ids == o, pattern_ref[o].astype(jnp.float32), extra)
    extra = extra.astype(jnp.bfloat16)
    for k in range(spans):
        q_refs[k][rows:] = extra

    lanes = lax.broadcasted_iota(jnp.int32, (1, rows), 1)
    row_ids = lax.broadcasted_iota(jnp.int32, (rows, HEAD_SIZE), 0)

    def count(span, step_row, step_col):
        return counts_ref[span, at[0] + step_row, at[1] + step_col]

    for other in range(spans):
        keep_ref[other] = jnp.where(row_ids < count(other, 0, 0), 1.0, 0.0)
        for t, way in enumerate(ways):
            if way is None:
                near = count(other, 0, 0)
            else:
                step = partner(at[way[0]], sizes[way[0]], way[1])
                near = count(other, *((step, 0) if way[0] == 0 else (0, step)))
                near = jnp.where(step == 0, 0, near)
            for span in range(other, spans):
                seen = jnp.where(mask_ref[span, other] > 0, near, 0)
                bias_ref[span, t : t + 1, other * rows : (other + 1) * rows] = jnp.where(
                    lanes < seen, 0.0, DEAD
                )

    copies[3].wait()
    for k in range(spans):
        for part in range(2):
            start = pl.multiple_of(part * kv_width + (me ^ k) * HEAD_SIZE, HEAD_SIZE)
            kv_refs[k][part] = kv_ref[:, pl.ds(start, HEAD_SIZE)]
    copies[4].wait()
    for k in range(spans):
        q_refs[k][:rows] = q_ref[:, pl.ds(pl.multiple_of((me ^ k) * width, HEAD_SIZE), width)]


def attend(spans, sizes, ways, numbers, chosen, *refs):
    first, last = numbers[0] == 0, numbers[-1] == len(ways) - 1
    q_ref, refs = refs[0], refs[1:]
    tile_refs, refs = dict(zip(numbers, refs, strict=False)), refs[len(numbers) :]
    (bias_ref, keep_ref), refs = refs[:2], refs[2:]
    if not first:
        (top_in, sum_in, acc_in), refs = refs[:3], refs[3:]
    if last:
        (out_ref,), refs = refs[:1], refs[1:]
    else:
        (top_ref, sum_ref, acc_ref), refs = refs[:3], refs[3:]
    (score_ref,) = refs
    me = lax.axis_index("span")
    tok_rows = q_ref.shape[1] - EXTRA
    groups = q_ref.shape[2] // HEAD_SIZE
    factor = HEAD_SIZE ** (-0.5) * math.log2(math.e)

    def pattern_rows(n):
        if ways[n] is None:
            return 0, 0
        base = 1 + 2 * ways[n][0]
        return base, base + 1

    steps = {
        n: None
        if ways[n] is None
        else partner(lax.axis_index(("ty", "tx")[ways[n][0]]), sizes[ways[n][0]], ways[n][1])
        for n in numbers
    }

    def bias_of(span, used):
        extra = q_ref[me ^ span, tok_rows:, :HEAD_SIZE].astype(jnp.float32)
        parts = []
        for n in used:
            step = steps[n]
            low, high = pattern_rows(n)
            chosen = extra[low : low + 1]
            if step is not None:
                chosen = jnp.where(step > 0, extra[high : high + 1], chosen)
            closed = jnp.where(chosen > 0, 0.0, DEAD)
            for other in range(span + 1):
                lanes = slice(other * tok_rows, (other + 1) * tok_rows)
                parts.append(bias_ref[span, n : n + 1, lanes] + closed)
        return jnp.concatenate(parts, axis=1)

    def gathered(span, part, used):
        return jnp.concatenate([t[me ^ o, part] for t in map(tile_refs.get, used) for o in range(span + 1)], axis=0)

    def score(span, used):
        query = jnp.concatenate(
            [q_ref[me ^ span, :tok_rows, g * HEAD_SIZE : (g + 1) * HEAD_SIZE] for g in range(groups)],
            axis=0,
        )
        keys = gathered(span, 0, used)
        score_ref[span, :, : keys.shape[0]] = lax.dot_general(
            query, keys, (((1,), (1,)), ((), ())), preferred_element_type=jnp.float32
        )

    def weigh(span, used):
        if used:
            values = gathered(span, 1, used)
            bias = bias_of(span, used)
            blocks = [slice(b, b + HEAD_SIZE) for b in range(0, values.shape[0], HEAD_SIZE)]
        for g in range(groups):
            rows = slice(g * tok_rows, (g + 1) * tok_rows)
            shape = (tok_rows, HEAD_SIZE)
            if used:
                before = jnp.full(shape, DEAD, jnp.float32) if first else top_in[span, rows]
                top = before
                for lanes in blocks:
                    top = jnp.maximum(top, score_ref[span, rows, lanes] + bias[:, lanes])
                top = jnp.broadcast_to(jnp.max(top, axis=1, keepdims=True), shape)
                total, weights = jnp.zeros(shape, jnp.float32), []
                for lanes in blocks:
                    weight = jnp.exp2((score_ref[span, rows, lanes] + bias[:, lanes] - top) * factor)
                    total = total + weight
                    weights.append(weight.astype(jnp.bfloat16))
                result = jnp.dot(
                    jnp.concatenate(weights, axis=1), values, preferred_element_type=jnp.float32
                )
                if not first:
                    fade = jnp.exp2((before - top) * factor)
                    total = total + sum_in[span, rows] * fade
                    result = result + acc_in[span, rows] * fade
            else:
                top, total, result = top_in[span, rows], sum_in[span, rows], acc_in[span, rows]
            if not last:
                top_ref[span, rows], sum_ref[span, rows], acc_ref[span, rows] = top, total, result
                continue
            share = 1.0 / jnp.sum(total, axis=1, keepdims=True)
            result = result * jnp.where(top > 0.5 * DEAD, share, jnp.nan)
            out_ref[me ^ span, :, g * HEAD_SIZE : (g + 1) * HEAD_SIZE] = jnp.where(
                keep_ref[span] > 0, result, 0.0
            ).astype(jnp.bfloat16)

    def run(some, used):
        some = some[::-1]
        if used:
            score(some[0], used)
        for i, span in enumerate(some):
            if used and i + 1 < len(some):
                score(some[i + 1], used)
            weigh(span, used)

    members = {}
    for place in range(spans):
        members.setdefault(tuple(sorted(place ^ k for k in chosen)), []).append(place)
    borders = {
        tuple(n for n in numbers if ways[n] is None or has_partner(spot[ways[n][0]], sizes, ways[n]))
        for spot in itertools.product(*map(range, sizes))
    }
    for some, places in sorted(members.items()):
        for inside in sorted(borders):
            tests = [] if len(places) == spans else [[me == place for place in places]]
            if len(borders) > 1:
                tests += [[(steps[n] != 0) == (n in inside)] for n in numbers if steps[n] is not None]
            case = functools.partial(run, some, inside)
            if tests:
                tests = [functools.reduce(jnp.logical_or, test) for test in tests]
                pl.when(functools.reduce(jnp.logical_and, tests))(case)
            else:
                case()


def collect(spans, *refs):
    for k in range(spans):
        refs[spans][k] = refs[k][...]


def copy(own_ref, after_ref, copy_ref):
    copy_ref[...] = own_ref[...]


def join(places, *refs):
    me = lax.axis_index("span")
    out_ref = refs[-1]
    for k, ref in zip(places, refs, strict=False):
        width = ref.shape[1]
        start = pl.multiple_of((me ^ k) * width, HEAD_SIZE)
        out_ref[:, pl.ds(start, width)] = ref[...]


def shards(queries, key_value, pattern, counts, span_mask):
    spans, ty_count, tx_count = (lax.axis_size(a) for a in ("span", "ty", "tx"))
    tok_rows = queries.shape[3]
    kv_heads = key_value.shape[4] // (2 * HEAD_SIZE)
    assert kv_heads == spans and spans & (spans - 1) == 0
    width = queries.shape[4] // spans
    groups = width // HEAD_SIZE
    bf16 = jnp.bfloat16
    params = pltpu.CompilerParams(vmem_limit_bytes=VMEM_LIMIT)

    def exchange(block, k):
        return lax.ppermute(block, "span", [(i, i ^ k) for i in range(spans)])

    sizes = (ty_count, tx_count)
    order = sorted(range(1, spans), key=lambda k: -bin(k).count("1"))

    swaps = [
        (dim, first, pairs) for dim in (0, 1) for first, pairs in enumerate(pairings(sizes[dim]))
    ]
    ways = (None, *((dim, first) for dim, first, _ in swaps))
    piece = jax.ShapeDtypeStruct((2, tok_rows, HEAD_SIZE), bf16)
    pieces = pl.pallas_call(
        functools.partial(split, spans, sizes, ways),
        out_shape=[piece] * spans
        + [jax.ShapeDtypeStruct((tok_rows + EXTRA, width), bf16)] * spans
        + [
            jax.ShapeDtypeStruct((spans, 8, spans * tok_rows), jnp.float32),
            jax.ShapeDtypeStruct((spans, tok_rows, HEAD_SIZE), jnp.float32),
        ],
        in_specs=[pl.BlockSpec(memory_space=pltpu.HBM)] * 5,
        out_specs=[vmem()] * (2 * spans + 2),
        scratch_shapes=[
            pltpu.SMEM((NEIGH,), jnp.int32),
            pltpu.SMEM(counts.shape, jnp.int32),
            pltpu.SMEM(span_mask.shape, jnp.int32),
            pltpu.VMEM((tok_rows, 2 * kv_heads * HEAD_SIZE), bf16),
            pltpu.VMEM((tok_rows, spans * width), bf16),
            pltpu.SemaphoreType.DMA((5,)),
        ],
        compiler_params=params,
        name="split",
    )(
        *(
            pltpu.with_memory_space_constraint(x, pltpu.HBM)
            for x in (
                pattern.reshape(NEIGH),
                counts,
                span_mask,
                key_value.reshape(tok_rows, -1),
                queries.reshape(tok_rows, -1),
            )
        )
    )
    kv_pieces, q_pieces, masks = pieces[:spans], pieces[spans : 2 * spans], pieces[2 * spans :]

    column = [kv_pieces[0]] + [None] * (spans - 1)
    for k in order:
        column[k] = exchange(kv_pieces[k], k)
    own = jnp.stack(column)
    q_here = [q_pieces[0]] + [None] * (spans - 1)
    for k in order:
        q_here[k] = exchange(q_pieces[k], k)

    sizes = (ty_count, tx_count)
    rows = groups * tok_rows
    own_copy = pl.pallas_call(
        copy,
        out_shape=jax.ShapeDtypeStruct(own.shape, bf16),
        in_specs=[vmem()] * 2,
        out_specs=vmem(),
        compiler_params=params,
        cost_estimate=SMALL,
        name="copy",
    )(own, q_here[1])
    q_all = pl.pallas_call(
        functools.partial(collect, spans),
        out_shape=jax.ShapeDtypeStruct((spans, *q_here[0].shape), bf16),
        in_specs=[vmem()] * spans,
        out_specs=vmem(),
        compiler_params=params,
        cost_estimate=SMALL,
        name="collect",
    )(*q_here)
    tiles = [own] + [swap(own if dim else own_copy, sizes, dim, pairs) for dim, _, pairs in swaps]
    kept = jax.ShapeDtypeStruct((spans, rows, HEAD_SIZE), jnp.float32)
    result = jax.ShapeDtypeStruct((spans, tok_rows, width), bf16)

    def stage(start, stop, chosen, state, flops, name):
        numbers = tuple(range(start, stop))
        last = stop == len(tiles)
        given = (q_all, *tiles[start:stop], *masks, *state)
        return pl.pallas_call(
            functools.partial(attend, spans, sizes, ways, numbers, chosen),
            out_shape=[result] if last else [kept] * 3,
            in_specs=[vmem()] * len(given),
            out_specs=[vmem()] * (1 if last else 3),
            scratch_shapes=[pltpu.VMEM((spans, rows, spans * len(numbers) * tok_rows), jnp.float32)],
            compiler_params=params,
            cost_estimate=pl.CostEstimate(flops=flops, bytes_accessed=4_000_000, transcendentals=0),
            name=name,
        )(*given)

    state = ()
    cut = [0] + [n for n in CUTS if n < len(tiles)] + [len(tiles)]
    for start, stop in zip(cut[:-2], cut[1:-1], strict=True):
        flops = OWN_FLOPS if start == 0 else LATER_FLOPS
        state = stage(start, stop, range(spans), state, flops, f"attend_{start}")
    outs = [None] * spans
    parts = [tuple(range(spans))]
    for i, part in enumerate(parts):
        done = stage(cut[-2], cut[-1], part, state, LATER_FLOPS, f"attend_last_{i}")[0]
        for k in part:
            outs[k] = done[k]

    home = [outs[0]] + [None] * (spans - 1)
    places = [0, *range(2, spans), 1] if spans > 2 else list(range(spans))
    for k in order:
        home[k] = exchange(outs[k], k)
    attended = pl.pallas_call(
        functools.partial(join, places),
        out_shape=jax.ShapeDtypeStruct((tok_rows, spans * width), bf16),
        in_specs=[vmem()] * spans,
        out_specs=vmem(),
        compiler_params=params,
        name="join",
    )(*(home[k] for k in places))
    return attended.reshape(1, 1, 1, tok_rows, -1)


def solution(mesh):
    return jax.shard_map(
        shards,
        mesh=mesh,
        in_specs=(
            P("span", "ty", "tx", None, None),
            P("span", "ty", "tx", None, None),
            P("span", "ty", "tx", None),
            P(),
            P(),
        ),
        out_specs=P("span", "ty", "tx", None, None),
        check_vma=False,
    )
```
